32 devices in a mesh: clus: 8 (over z, core), grp: 4 (over y, x).
Axes of the slice: x: 2, y: 2, z: 4, core: 2. Of those that a mesh axis runs over, the one named last changes fastest.
Arguments:
- features: bfloat16 [8, 4, 1024, 256], P('clus', 'grp'), may hold values from -6 to 6
- history: bfloat16 [8, 4, 1024, 256], P('clus', 'grp'), may hold values from -6 to 6
- aux_history: bfloat16 [8, 4, 1024, 256], P('clus', 'grp'), may hold values from -0.625 to 0.625
- tile_values: bfloat16 [8, 4, 8, 4, 128, 128], P('clus', 'grp'), may hold values from -0.25 to 0.25
- tile_sources: int32 [8, 4, 8, 4], P('clus', 'grp'), may hold values from 0 to 15, as said below
- send_list: int32 [8, 4, 4, 2], P('clus', 'grp'), may hold values from 0 to 8, as said below
- event_bins: int32 [8, 4, 1024], P('clus', 'grp'), may hold values from 0 to 31
- event_flags: int32 [8, 4, 1024], P('clus', 'grp'), may hold values 0 or 1
- neigh_first: bfloat16 [256, 256], replicated, may hold values from -0.375 to 0.375
- self_first: bfloat16 [256, 256], replicated, may hold values from -0.375 to 0.375
- neigh_second: bfloat16 [256, 256], replicated, may hold values from -0.375 to 0.375
- self_second: bfloat16 [256, 256], replicated, may hold values from -0.375 to 0.375
- hazard_weight: bfloat16 [256, 32], replicated, may hold values from -0.375 to 0.375
Outputs:
- new_history: bfloat16 [8, 4, 1024, 256], P('clus', 'grp')
- grad_hidden: bfloat16 [8, 4, 1024, 256], P('clus', 'grp')
- new_aux: bfloat16 [8, 4, 1024, 256], P('clus', 'grp')
- grad_neigh_first: float32 [256, 256], replicated
- grad_self_first: float32 [256, 256], replicated
- grad_neigh_second: float32 [256, 256], replicated
- grad_self_second: float32 [256, 256], replicated
- grad_hazard: float32 [256, 32], replicated
- loss: float32 [], replicated
The draws below stay inside these ranges and needn't reach their ends.
Inputs may be any that keep to these rules, and one draw needn't show every extreme that they name: `send_list`: entry [c, g, p, s] names the block of device (c, g) sent to device (c, p) in slot s, or 8 for an empty slot; live slots come first in a list; a device's list to itself is empty; every other list has one or two live slots, and every device has at least one full list and at least one list with a single live slot. `tile_sources`: indexes the device's source table; never an empty slot; every live received slot is read by some tile.
All inputs are finite; a program needn't handle non-finite values. No bound on the sum of `event_flags` on one device may be relied on, other than what follows from the above.
Results may differ from the reference program's by a relative error of at most 0.014.
Values may be sent and summed in bfloat16 or wider, within the bound.
No kernel may reach another device: no remote copies, remote signals or barrier semaphores. Data moves between devices by JAX's collectives and lax.ppermute only.
A program may use at most 64 MiB of HBM per device.

```python
import jax
import jax.numpy as jnp
from jax import lax

D = 256
TB = 32
BLK = 128
NB = 8
K = 4
S = 2
ROWS = 1024
N_CLUS = 8
N_GRP = 4


def routing_tables(key):
    routing_key = jax.random.fold_in(key, 7)
    key_count, key_block, key_pick, key_order = jax.random.split(routing_key, 4)
    device_col = jnp.arange(N_GRP, dtype=jnp.int32)[:, None]
    peer_row = jnp.arange(N_GRP, dtype=jnp.int32)[None, :]
    counts = jax.random.randint(key_count, (N_CLUS, N_GRP, N_GRP), 1, S + 1)
    counts = jnp.where(peer_row == (device_col + 2) % N_GRP, 1, counts)
    counts = jnp.where(peer_row == (device_col + 1) % N_GRP, S, counts)
    counts = jnp.where(peer_row == device_col, 0, counts)
    blocks = jax.random.randint(key_block, (N_CLUS, N_GRP, N_GRP, S), 0, NB)
    slot_index = jnp.arange(S, dtype=jnp.int32)
    routing = jnp.where(slot_index < counts[..., None], blocks, NB).astype(jnp.int32)
    live_slot = (jnp.swapaxes(routing, 1, 2) < NB).reshape(N_CLUS, N_GRP, N_GRP * S)
    tile_total = NB * K
    drawn = jax.random.randint(key_pick, (N_CLUS, N_GRP, tile_total), 0, NB + N_GRP * S)
    remote = jnp.clip(drawn - NB, 0, N_GRP * S - 1)
    drawn_live = (drawn >= NB) & jnp.take_along_axis(live_slot, remote, axis=2)
    fallback = jnp.where(drawn_live, drawn, drawn % NB)
    position = jnp.arange(tile_total, dtype=jnp.int32)
    cover_slot = jnp.broadcast_to(jnp.clip(position, 0, N_GRP * S - 1), (N_CLUS, N_GRP, tile_total))
    covering = (position < N_GRP * S) & jnp.take_along_axis(live_slot, cover_slot, axis=2)
    chosen = jnp.where(covering, NB + position, fallback)
    scores = jax.random.randint(key_order, (N_CLUS, N_GRP, tile_total), 0, 1 << 20) * tile_total + position
    ordering = jnp.argsort(scores, axis=2)
    chosen = jnp.take_along_axis(chosen, ordering, axis=2)
    return (routing, chosen.reshape(N_CLUS, N_GRP, NB, K).astype(jnp.int32))


def draw_send_list(key, part):
    return routing_tables(key)[0]


def draw_tile_sources(key, part):
    return routing_tables(key)[1]


def plant(values, key, least, top_value):
    longest = values.shape.index(max(values.shape))
    spots = []
    for shift in (0, 1):
        where = [jax.random.randint(jax.random.fold_in(key, axis), (), 0, length) for axis, length in enumerate(values.shape)]
        where[longest] = (where[longest] + shift) % values.shape[longest]
        spots.append(tuple(where))
    return values.at[spots[0]].set(least).at[spots[1]].set(top_value)


def levels(stream_key, extent, pieces, low, high):
    level, own = 1.0, jax.random.fold_in(stream_key, 6)
    for dim, parts in pieces:
        steps = jnp.exp(jax.random.uniform(jax.random.fold_in(own, dim), (parts,), jnp.float32, low / len(pieces), high / len(pieces)))
        level = level * jnp.repeat(steps, extent[dim] // parts).reshape([-1 if axis == dim else 1 for axis in range(len(extent))])
    return level


def noise(rng, dims, scale, reach, cuts=(), held_as=jnp.bfloat16):
    values = scale * jax.random.normal(rng, dims, jnp.float32)
    if cuts:
        values = values * levels(rng, dims, cuts, -0.22, 0.18)
    return jnp.clip(values, -reach, reach).astype(held_as)


def setup_inputs(seed: int = 0) -> dict:
    keys = jax.random.split(jax.random.key(seed), 14)
    return {
        "features": noise(keys[0], (N_CLUS, N_GRP, ROWS, D), 1.0, 6.0, ((0, 8), (1, 4))),
        "history": noise(keys[1], (N_CLUS, N_GRP, ROWS, D), 1.0, 6.0, ((0, 8), (1, 4))),
        "aux_history": noise(keys[2], (N_CLUS, N_GRP, ROWS, D), 0.1, 0.625, ((0, 8), (1, 4))),
        "tile_values": noise(keys[3], (N_CLUS, N_GRP, NB, K, BLK, BLK), (K * BLK) ** -0.5, 0.25, ((0, 8), (1, 4))),
        "tile_sources": draw_tile_sources(jax.random.fold_in(keys[13], 71), 0),
        "send_list": draw_send_list(jax.random.fold_in(keys[13], 71), 0),
        "event_bins": plant(jax.random.randint(keys[6], (N_CLUS, N_GRP, ROWS), 0, TB), jax.random.fold_in(keys[6], 1), 0, TB - 1).astype(jnp.int32),
        "event_flags": plant((jax.random.randint(keys[7], (N_CLUS, N_GRP, ROWS), 0, 10) < 7).astype(jnp.int32), jax.random.fold_in(keys[7], 1), 0, 1),
        "neigh_first": noise(keys[8], (D, D), D ** -0.5, 0.375),
        "self_first": noise(keys[9], (D, D), D ** -0.5, 0.375),
        "neigh_second": noise(keys[10], (D, D), D ** -0.5, 0.375),
        "self_second": noise(keys[11], (D, D), D ** -0.5, 0.375),
        "hazard_weight": noise(keys[12], (D, TB), D ** -0.5, 0.375),
    }


def silu_slope(preact):
    logistic = jax.nn.sigmoid(preact)
    return logistic * (1.0 + preact * (1.0 - logistic))


def aggregate(source_table, sources, tile_vals):
    picked = source_table[sources]
    return jnp.einsum("bkij,bkjd->bid", tile_vals.astype(jnp.float32), picked.astype(jnp.float32))


def spread_back(tile_vals, sources, grad_blocks, table_size):
    contribution = jnp.einsum("bkij,bid->bkjd", tile_vals.astype(jnp.float32), grad_blocks.astype(jnp.float32))
    flattened = contribution.reshape((-1,) + contribution.shape[2:])
    return jax.ops.segment_sum(flattened, sources.reshape(-1), num_segments=table_size)


def transpose_dot(former, latter):
    return jnp.dot(former.T, latter, preferred_element_type=jnp.float32)


def reference(features, history, aux_history, tile_values, tile_sources, send_list, event_bins, event_flags, neigh_first, self_first, neigh_second, self_second, hazard_weight):
    def one_batch(packed):
        feat, past, aux_rows, tile_vals, sources, routing, event_bin, event_flag = packed
        group_size, node_rows, feat_width = feat.shape
        block_count = tile_vals.shape[1]
        block_rows = tile_vals.shape[3]
        slot_count = routing.shape[2]
        row_scale = 1.0 / (group_size * node_rows)
        flat_rows = group_size * node_rows

        def received(values):
            blocks = values.reshape(group_size, block_count, block_rows, feat_width)
            clamped = jnp.minimum(routing, block_count - 1)
            outbound = jax.vmap(lambda block_set, index_set: block_set[index_set])(blocks, clamped)
            outbound = jnp.where((routing < block_count)[..., None, None], outbound, jnp.zeros((), values.dtype))
            return jnp.swapaxes(outbound, 0, 1)

        def table_of(values, incoming):
            own = values.reshape(group_size, block_count, block_rows, feat_width)
            return jnp.concatenate([own, incoming.reshape(group_size, group_size * slot_count, block_rows, feat_width)], axis=1)

        agg_first = jax.vmap(aggregate)(table_of(feat, received(feat)), sources, tile_vals).astype(jnp.bfloat16).reshape(flat_rows, feat_width)
        feat_flat = feat.reshape(flat_rows, feat_width)
        pre_first = jnp.dot(agg_first, neigh_first, preferred_element_type=jnp.float32) + jnp.dot(feat_flat, self_first, preferred_element_type=jnp.float32)
        hidden_first = jax.nn.silu(pre_first).astype(jnp.bfloat16)
        agg_second = jax.vmap(aggregate)(table_of(hidden_first, received(past)), sources, tile_vals).astype(jnp.bfloat16).reshape(flat_rows, feat_width)
        pre_second = jnp.dot(agg_second, neigh_second, preferred_element_type=jnp.float32) + jnp.dot(hidden_first, self_second, preferred_element_type=jnp.float32)
        hidden_second = jax.nn.silu(pre_second).astype(jnp.bfloat16)
        logits = jnp.dot(hidden_second, hazard_weight, preferred_element_type=jnp.float32)
        bins_col = event_bin.reshape(flat_rows, 1)
        flag_col = event_flag.reshape(flat_rows, 1).astype(jnp.float32)
        step_row = jnp.arange(logits.shape[1], dtype=jnp.int32)[None, :]
        counted = step_row <= bins_col
        at_event = (step_row == bins_col).astype(jnp.float32)
        node_loss = jnp.sum(jnp.where(counted, jax.nn.softplus(logits), 0.0), axis=1) - flag_col[:, 0] * jnp.sum(at_event * logits, axis=1)
        batch_loss = jnp.sum(node_loss) * row_scale
        grad_logits = (jnp.where(counted, jax.nn.sigmoid(logits), 0.0) - flag_col * at_event).astype(jnp.bfloat16)
        grad_hazard = transpose_dot(hidden_second, grad_logits) * row_scale
        grad_pre_second = (jnp.dot(grad_logits, hazard_weight.T, preferred_element_type=jnp.float32) * silu_slope(pre_second)).astype(jnp.bfloat16)
        grad_neigh_second = transpose_dot(agg_second, grad_pre_second) * row_scale
        grad_self_second = transpose_dot(hidden_first, grad_pre_second) * row_scale
        grad_agg = jnp.dot(grad_pre_second, neigh_second.T, preferred_element_type=jnp.float32).astype(jnp.bfloat16)
        table_size = block_count + group_size * slot_count
        grad_table = jax.vmap(lambda tv, sr, gb: spread_back(tv, sr, gb, table_size))(tile_vals, sources, grad_agg.reshape(group_size, block_count, block_rows, feat_width))
        sent_back = grad_table[:, block_count:].astype(jnp.bfloat16).reshape(group_size, group_size, slot_count, block_rows, feat_width)
        came_back = jnp.swapaxes(sent_back, 0, 1).astype(jnp.float32)
        selector = (routing[..., None] == jnp.arange(block_count, dtype=jnp.int32)).astype(jnp.float32)
        new_aux = jnp.einsum("gpsj,gpsid->gjid", selector, came_back).astype(jnp.bfloat16).reshape(flat_rows, feat_width)
        grad_total = grad_table[:, :block_count].reshape(flat_rows, feat_width) + jnp.dot(grad_pre_second, self_second.T, preferred_element_type=jnp.float32) + aux_rows.reshape(flat_rows, feat_width).astype(jnp.float32)
        grad_hidden = grad_total.astype(jnp.bfloat16)
        grad_pre_first = (grad_total * silu_slope(pre_first)).astype(jnp.bfloat16)
        grad_neigh_first = transpose_dot(agg_first, grad_pre_first) * row_scale
        grad_self_first = transpose_dot(feat_flat, grad_pre_first) * row_scale
        shape_back = (group_size, node_rows, feat_width)
        return (hidden_first.reshape(shape_back), grad_hidden.reshape(shape_back), new_aux.reshape(shape_back), grad_neigh_first, grad_self_first, grad_neigh_second, grad_self_second, grad_hazard, batch_loss)

    results = lax.map(one_batch, (features, history, aux_history, tile_values, tile_sources, send_list, event_bins, event_flags))
    return (results[0], results[1], results[2], jnp.sum(results[3], axis=0), jnp.sum(results[4], axis=0), jnp.sum(results[5], axis=0), jnp.sum(results[6], axis=0), jnp.sum(results[7], axis=0), jnp.sum(results[8]))
```

```python
import functools

import jax
import jax.numpy as jnp
from jax import lax
from jax.experimental import pallas as pl
from jax.experimental.pallas import tpu as pltpu
from jax.sharding import PartitionSpec as P

BF16 = jnp.bfloat16
F32 = jnp.float32
VMEM = pl.BlockSpec(memory_space=pltpu.VMEM)
SMEM = pl.BlockSpec(memory_space=pltpu.SMEM)
ANY = pl.BlockSpec(memory_space=pl.ANY)
CORES = 2


def dot(former, latter):
    return jnp.dot(former, latter, preferred_element_type=F32)


def transpose_dot(former, latter):
    return lax.dot_general(former, latter, (((0,), (0,)), ((), ())), preferred_element_type=F32)


def dot_by_transpose(former, latter):
    return lax.dot_general(former, latter, (((1,), (1,)), ((), ())), preferred_element_type=F32)


def partner(index, step, count):
    if count & (count - 1) == 0:
        return index ^ step, index ^ step
    return (index + step) % count, (index + count - step) % count


def pack_kernel(peers, slots, blocks, send, feat, past, *refs):
    outs, sems = refs[:-1], refs[-1]
    g = lax.axis_index("grp")
    copies = []
    for step in range(1, peers):
        peer, _ = partner(g, step, peers)
        for s in range(slots):
            block = jnp.minimum(send[s, peer], blocks - 1)
            for which, values in enumerate((feat, past)):
                copies.append(
                    pltpu.make_async_copy(
                        values.at[block],
                        outs[which * (peers - 1) + step - 1].at[s],
                        sems.at[len(copies)],
                    )
                )
    for copy in copies:
        copy.start()
    for copy in copies:
        copy.wait()


def main_kernel(dims, sources, *refs):
    peers, slots, blocks, picks, rows, width, bins_count, devices, clus_count, pay_rows = dims
    inc = peers - 1
    (feat, tiles, aux, bins, flags, wn1, ws1, wn2, ws2, hw), refs = refs[:10], refs[10:]
    feat_in, past_in, refs = refs[:inc], refs[inc : 2 * inc], refs[2 * inc :]
    (hidden_out, grad_hidden_out, keep, send), refs = refs[:4], refs[4:]
    back_out, refs = refs[:inc], refs[inc:]
    (table1, table2, agg1, agg2, slope1, gps, gagg, gtab, gpf, pay, sems) = refs
    g = lax.axis_index("grp")
    core = lax.axis_index("clus") % CORES
    device = lax.axis_index("clus") * peers + g
    nodes = blocks * rows
    scale = 1.0 / (nodes * peers)
    copies = []
    for step in range(1, peers):
        _, origin = partner(g, step, peers)
        slot = pl.ds(blocks + origin * slots, slots)
        copies.append(pltpu.make_async_copy(feat_in[step - 1], table1.at[slot], sems.at[2 * step - 2]))
        copies.append(pltpu.make_async_copy(past_in[step - 1], table2.at[slot], sems.at[2 * step - 1]))
    for copy in copies:
        copy.start()
    table1[pl.ds(0, blocks)] = feat[...]
    for copy in copies:
        copy.wait()

    def gathered(table, b):
        return jnp.concatenate([table[sources[k, b]] for k in range(picks)], axis=0)

    def tile_row(b):
        return jnp.concatenate([tiles[b, k] for k in range(picks)], axis=1)

    pair = 2
    span = pair * rows

    def aggregate(table, result):
        @pl.loop(0, blocks)
        def _(b):
            result[b] = dot(tile_row(b), gathered(table, b)).astype(BF16)

    def two(ref, i):
        return ref[pl.ds(i * pair, pair)].reshape(span, width)

    aggregate(table1, agg1)

    @pl.loop(0, blocks // pair)
    def _(i):
        both = jnp.concatenate([two(agg1, i), two(table1, i)], axis=1)
        pre = dot(both, jnp.concatenate([wn1[...], ws1[...]], axis=0))
        gate = 0.5 * jnp.tanh(0.5 * pre) + 0.5
        value = pre * gate
        slope1[pl.ds(i * span, span)] = gate + value * (1.0 - gate)
        hidden = value.astype(BF16).reshape(pair, rows, width)
        table2[pl.ds(i * pair, pair)] = hidden
        hidden_out[pl.ds(i * pair, pair)] = hidden

    aggregate(table2, agg2)
    head = hw[...]
    step_col = lax.broadcasted_iota(jnp.int32, (bins_count, span), 0)

    def second(i, carry):
        loss, ghw = carry
        both = jnp.concatenate([two(agg2, i), two(table2, i)], axis=1)
        pre = dot(both, jnp.concatenate([wn2[...], ws2[...]], axis=0))
        gate = 0.5 * jnp.tanh(0.5 * pre) + 0.5
        value = pre * gate
        slope = gate + value * (1.0 - gate)
        hidden = value.astype(BF16)
        logits = dot_by_transpose(head, hidden)
        bin_row = bins[i]
        flag_row = flags[i].astype(F32)
        counted = step_col <= bin_row
        event = jnp.where(step_col == bin_row, flag_row, 0.0)
        tail = jnp.exp(-jnp.abs(logits))
        soft = jnp.maximum(logits, 0.0) + jnp.log1p(tail)
        loss = loss + jnp.where(counted, soft, 0.0) - event * logits
        chance = jnp.where(logits >= 0.0, 1.0, tail) / (1.0 + tail)
        glog = (jnp.where(counted, chance, 0.0) - event).astype(BF16)
        ghw = ghw + dot(glog, hidden)
        grad_pre = (transpose_dot(glog, head) * slope).astype(BF16)
        gps[pl.ds(i * span, span)] = grad_pre
        gagg[pl.ds(i * pair, pair)] = (
            dot_by_transpose(grad_pre, wn2[...]).astype(BF16).reshape(pair, rows, width)
        )
        own = dot_by_transpose(grad_pre, ws2[...]) + two(aux, i).astype(F32)
        gtab[pl.ds(i * pair, pair)] = own.reshape(pair, rows, width)
        return loss, ghw

    loss, ghw = lax.fori_loop(
        0,
        blocks // pair,
        second,
        (jnp.zeros((bins_count, span), F32), jnp.zeros((bins_count, width), F32)),
    )
    gtab[pl.ds(blocks, peers * slots)] = jnp.zeros((peers * slots, rows, width), F32)

    @pl.loop(0, blocks)
    def _(b):
        spread = transpose_dot(tile_row(b), gagg[b])
        for k in range(picks):
            gtab[sources[k, b]] += spread[k * rows : (k + 1) * rows]

    for step in range(1, peers):
        _, origin = partner(g, step, peers)
        for s in range(slots):
            back_out[step - 1][s] = gtab[blocks + origin * slots + s].astype(BF16)

    @pl.loop(0, blocks // pair)
    def _(i):
        total = gtab[pl.ds(i * pair, pair)]
        grad_hidden_out[pl.ds(i * pair, pair)] = total.astype(BF16)
        gpf[pl.ds(i * span, span)] = (
            total.reshape(span, width) * slope1[pl.ds(i * span, span)]
        ).astype(BF16)

    def weight_grads(at, left, right, grads):
        pay[pl.ds(at, width)] = (
            transpose_dot(left.reshape(nodes, width), grads[...]) * scale
        ).astype(BF16)
        pay[pl.ds(at + width, width)] = (
            transpose_dot(right.reshape(nodes, width), grads[...]) * scale
        ).astype(BF16)

    weight_grads(0, agg1[...], table1[pl.ds(0, blocks)], gpf)
    weight_grads(2 * width, agg2[...], table2[pl.ds(0, blocks)], gps)
    part = jnp.sum(loss) * scale
    high = part.astype(BF16).astype(F32)
    tail_rows = pay_rows - 4 * width - bins_count
    lane = lax.broadcasted_iota(jnp.int32, (tail_rows, width), 0) * width + lax.broadcasted_iota(
        jnp.int32, (tail_rows, width), 1
    )
    loss_rows = jnp.where(lane == 2 * device, high, 0.0) + jnp.where(
        lane == 2 * device + 1, part - high, 0.0
    )
    pay[pl.ds(4 * width, bins_count)] = (ghw * scale).astype(BF16)
    pay[pl.ds(4 * width + bins_count, tail_rows)] = loss_rows.astype(BF16)
    half = pay_rows // CORES
    keep[...] = pay[pl.ds(pl.multiple_of(core * half, 16), half)]
    send[...] = pay[pl.ds(pl.multiple_of((1 - core) * half, 16), half)]


def split_kernel(peers, kept, came, own, *outs):
    g = lax.axis_index("grp")

    def chunk(p):
        return (kept[p].astype(F32) + came[p].astype(F32)).astype(BF16)

    own[...] = chunk(g)
    for step in range(1, peers):
        peer, _ = partner(g, step, peers)
        outs[step - 1][...] = chunk(peer)


def add_kernel(*refs):
    total = refs[0][...].astype(F32)
    for ref in refs[1:-1]:
        total = total + ref[...].astype(F32)
    refs[-1][...] = total.astype(BF16)


def join_kernel(peers, own, *refs):
    out = refs[-1]
    g = lax.axis_index("grp")
    out[g] = own[...]
    for step in range(1, peers):
        _, origin = partner(g, step, peers)
        out[origin] = refs[step - 1][...]


def finish_kernel(dims, mine, other, *outs):
    width, bins_count, devices, pay_rows = dims
    pay = outs[-1]
    half = pay_rows // CORES
    core = lax.axis_index("clus") % CORES
    pay[pl.ds(pl.multiple_of(core * half, 16), half)] = mine[...]
    pay[pl.ds(pl.multiple_of((1 - core) * half, 16), half)] = other[...]
    for i in range(4):
        outs[i][...] = pay[pl.ds(i * width, width)].astype(F32)
    outs[4][...] = pay[pl.ds(4 * width, bins_count)].astype(F32)
    loss_rows = pay[pl.ds(4 * width + bins_count, pay_rows - 4 * width - bins_count)].astype(F32)
    outs[5][0, 0] = jnp.sum(loss_rows)


def add_aux_kernel(peers, slots, blocks, terms, send, *refs):
    add_kernel(*refs[:terms], refs[-3])
    back, out, total = refs[terms:-3], refs[-2], refs[-1]
    g = lax.axis_index("grp")
    total[...] = jnp.zeros_like(total)
    for step in range(1, peers):
        peer, _ = partner(g, step, peers)
        for s in range(slots):
            total[send[s, peer]] += back[step - 1][s].astype(F32)
    out[...] = total[pl.ds(0, blocks)].astype(BF16)


def shards(
    clus_count,
    peers,
    features,
    history,
    aux_history,
    tile_values,
    tile_sources,
    send_list,
    event_bins,
    event_flags,
    neigh_first,
    self_first,
    neigh_second,
    self_second,
    hazard_weight,
):
    blocks, picks, rows = tile_values.shape[2:5]
    width = features.shape[3]
    slots = send_list.shape[3]
    bins_count = hazard_weight.shape[1]
    devices = clus_count * peers
    chips_z = clus_count // CORES
    inc = peers - 1
    used = 4 * width + bins_count + -(-2 * devices // width)
    pay_rows = -(-used // (16 * CORES * peers)) * 16 * CORES * peers
    half = pay_rows // CORES
    chunk = half // peers
    block_shape = (blocks, rows, width)
    slot_shape = (slots, rows, width)
    routing = send_list[0, 0].T
    feat = features.reshape(block_shape)
    past = history.reshape(block_shape)
    params = pltpu.CompilerParams(vmem_limit_bytes=20 << 20)
    small = pltpu.CompilerParams(vmem_limit_bytes=4 << 20)

    def shape(dims, dtype=BF16):
        return jax.ShapeDtypeStruct(dims, dtype)

    def grp_pairs(step):
        return [(i, partner(i, step, peers)[0]) for i in range(peers)]

    def over_grp(value, step):
        return lax.ppermute(value, "grp", grp_pairs(step))

    def over_z(value, step):
        pairs = [
            (z * CORES + c, partner(z, step, chips_z)[0] * CORES + c)
            for z in range(chips_z)
            for c in range(CORES)
        ]
        return lax.ppermute(value, "clus", pairs)

    def over_core(value):
        return lax.ppermute(value, "clus", [(i, i ^ 1) for i in range(clus_count)])

    packed = pl.pallas_call(
        functools.partial(pack_kernel, peers, slots, blocks),
        out_shape=[shape(slot_shape)] * (2 * inc),
        in_specs=[SMEM, ANY, ANY],
        out_specs=[VMEM] * (2 * inc),
        scratch_shapes=[pltpu.SemaphoreType.DMA((2 * inc * slots,))],
        compiler_params=small,
        name="pack",
    )(routing, feat, past)
    feat_in = [over_grp(packed[i], i + 1) for i in range(inc)]
    past_in = [over_grp(packed[inc + i], i + 1) for i in range(inc)]

    pair_shape = (blocks // 2, 1, 2 * rows)
    dims = (peers, slots, blocks, picks, rows, width, bins_count, devices, clus_count, pay_rows)
    nodes = blocks * rows
    table = blocks + peers * slots
    outs = pl.pallas_call(
        functools.partial(main_kernel, dims),
        out_shape=[shape(block_shape), shape(block_shape), shape((half, width)), shape((half, width))]
        + [shape(slot_shape)] * inc,
        in_specs=[SMEM] + [VMEM] * 10 + [ANY] * (2 * inc),
        out_specs=[VMEM] * (4 + inc),
        scratch_shapes=[
            pltpu.VMEM((table, rows, width), BF16),
            pltpu.VMEM((table, rows, width), BF16),
            pltpu.VMEM(block_shape, BF16),
            pltpu.VMEM(block_shape, BF16),
            pltpu.VMEM((nodes, width), F32),
            pltpu.VMEM((nodes, width), BF16),
            pltpu.VMEM(block_shape, BF16),
            pltpu.VMEM((table, rows, width), F32),
            pltpu.VMEM((nodes, width), BF16),
            pltpu.VMEM((pay_rows, width), BF16),
            pltpu.SemaphoreType.DMA((2 * inc,)),
        ],
        compiler_params=params,
        name="network",
    )(
        tile_sources[0, 0].T,
        feat,
        tile_values[0, 0],
        aux_history.reshape(block_shape),
        event_bins.reshape(pair_shape),
        event_flags.reshape(pair_shape),
        neigh_first,
        self_first,
        neigh_second,
        self_second,
        hazard_weight.T,
        *feat_in,
        *past_in,
    )
    hidden_first, grad_hidden, kept, sent = outs[:4]
    back = outs[4:]

    came = over_core(sent)
    parts = pl.pallas_call(
        functools.partial(split_kernel, peers),
        out_shape=[shape((chunk, width))] * peers,
        in_specs=[VMEM, VMEM],
        out_specs=[VMEM] * peers,
        compiler_params=small,
        name="split",
    )(kept.reshape(peers, chunk, width), came.reshape(peers, chunk, width))
    from_grp = [over_grp(parts[i], i) for i in range(1, peers)]
    came_back = [over_grp(back[i], i + 1) for i in range(inc)]

    def add(*values):
        return pl.pallas_call(
            add_kernel,
            out_shape=shape((chunk, width)),
            in_specs=[VMEM] * len(values),
            out_specs=VMEM,
            compiler_params=small,
            name="add",
        )(*values)

    mine = add(parts[0], *from_grp)
    terms = [mine] + [over_z(mine, i) for i in range(1, chips_z)]
    mine, new_aux = pl.pallas_call(
        functools.partial(add_aux_kernel, peers, slots, blocks, len(terms)),
        out_shape=[shape((chunk, width)), shape(block_shape)],
        in_specs=[SMEM] + [VMEM] * (len(terms) + inc),
        out_specs=[VMEM] * 2,
        scratch_shapes=[pltpu.VMEM((blocks + 1, rows, width), F32)],
        compiler_params=small,
        name="add_aux",
    )(routing, *terms, *came_back)
    others = [over_grp(mine, i) for i in range(1, peers)]
    joined = pl.pallas_call(
        functools.partial(join_kernel, peers),
        out_shape=shape((peers, chunk, width)),
        in_specs=[VMEM] * peers,
        out_specs=VMEM,
        compiler_params=small,
        name="join",
    )(mine, *others).reshape(half, width)
    other_half = over_core(joined)
    square = shape((width, width), F32)
    grads = pl.pallas_call(
        functools.partial(finish_kernel, (width, bins_count, devices, pay_rows)),
        out_shape=[square] * 4 + [shape((bins_count, width), F32), shape((1, 1), F32)],
        in_specs=[VMEM, VMEM],
        out_specs=[VMEM] * 5 + [SMEM],
        scratch_shapes=[pltpu.VMEM((pay_rows, width), BF16)],
        compiler_params=small,
        name="finish",
    )(joined, other_half)
    return (
        hidden_first.reshape(features.shape),
        grad_hidden.reshape(features.shape),
        new_aux.reshape(features.shape),
        *grads[:4],
        grads[4].T,
        grads[5][0, 0],
    )


def solution(mesh):
    split = P("clus", "grp")
    whole = P()
    return jax.shard_map(
        functools.partial(shards, mesh.shape["clus"], mesh.shape["grp"]),
        mesh=mesh,
        in_specs=(split,) * 8 + (whole,) * 5,
        out_specs=(split,) * 3 + (whole,) * 6,
        check_vma=False,
    )
```

```python
import functools

import jax
import jax.numpy as jnp
from jax import lax
from jax.experimental import pallas as pl
from jax.experimental.pallas import tpu as pltpu
from jax.sharding import PartitionSpec as P

BF16 = jnp.bfloat16
F32 = jnp.float32
VMEM = pl.BlockSpec(memory_space=pltpu.VMEM)
SMEM = pl.BlockSpec(memory_space=pltpu.SMEM)
HBM = pl.BlockSpec(memory_space=pltpu.HBM)
CORES = 2
PACK_LIMIT = 40 << 20
PREP_LIMIT = 4 << 20
AUX_FLOPS = 10**6


def dot(former, latter):
    return jnp.dot(former, latter, preferred_element_type=F32)


def transpose_dot(former, latter):
    return lax.dot_general(former, latter, (((0,), (0,)), ((), ())), preferred_element_type=F32)


def dot_by_transpose(former, latter):
    return lax.dot_general(former, latter, (((1,), (1,)), ((), ())), preferred_element_type=F32)


def partner(index, step, count):
    if count & (count - 1) == 0:
        return index ^ step, index ^ step
    return (index + step) % count, (index + count - step) % count


def pack_kernel(peers, slots, blocks, send, feat_in, past_in, *refs):
    outs, (token, lists, feat, past, sems) = refs[:-5], refs[-5:]
    g = lax.axis_index("grp")
    pairs = ((send, lists), (feat_in, feat), (past_in, past))
    copies = [pltpu.make_async_copy(src, dst, sems.at[i]) for i, (src, dst) in enumerate(pairs)]
    for copy in copies:
        copy.start()
    token[...] = jnp.zeros_like(token)
    copies[0].wait()
    for which, values in enumerate((feat, past)):
        copies[1 + which].wait()
        for step in range(1, peers):
            peer, _ = partner(g, step, peers)
            for s in range(slots):
                block = jnp.minimum(lists[s, peer], blocks - 1)
                outs[which * (peers - 1) + step - 1][s] = values[block]


def prepare_kernel(dims, feat_in, tiles_in, token, tiles, tiles_t, feat, feat_t, sems):
    blocks, picks, rows = dims
    whole = pltpu.make_async_copy(feat_in, feat, sems.at[0])
    copies = [
        pltpu.make_async_copy(tiles_in.at[b], tiles.at[b], sems.at[1 + b]) for b in range(blocks)
    ]
    for copy in [whole] + copies:
        copy.start()
    whole.wait()
    for b in range(blocks):
        feat_t[:, b * rows : (b + 1) * rows] = feat[b].T
    for b in range(blocks):
        copies[b].wait()
        for k in range(picks):
            tiles_t[b, k * rows : (k + 1) * rows] = tiles[b, k].T


def gathered(table, sources, b, picks):
    return jnp.concatenate([table[sources[k, b]] for k in range(picks)], axis=0)


def gate_of(pre):
    gate = 0.5 * jnp.tanh(0.5 * pre) + 0.5
    value = pre * gate
    return value, gate + value * (1.0 - gate)


def first_kernel(dims, sources_in, wn_in, ws_in, feat, tiles, *refs):
    peers, slots, blocks, picks, rows, width = dims
    inc = peers - 1
    feat_in, refs = refs[:inc], refs[inc:]
    (hidden_out, own2, slope1, agg_t, hidden_t), refs = refs[:5], refs[5:]
    table, sources, wn, ws, sems, out_sem = refs
    g = lax.axis_index("grp")
    listed = pltpu.make_async_copy(sources_in, sources, sems.at[0])
    weights = [
        pltpu.make_async_copy(wn_in, wn, sems.at[1]),
        pltpu.make_async_copy(ws_in, ws, sems.at[2]),
    ]
    for copy in [listed] + weights:
        copy.start()
    table[pl.ds(0, blocks)] = feat[...]
    for step in range(1, peers):
        _, origin = partner(g, step, peers)
        table[pl.ds(blocks + origin * slots, slots)] = feat_in[step - 1][...]
    listed.wait()
    aggs = []
    for b in range(blocks):
        row = jnp.concatenate([tiles[b, k] for k in range(picks)], axis=1)
        agg = dot(row, gathered(table, sources, b, picks)).astype(BF16)
        aggs.append(agg)
        agg_t[:, b * rows : (b + 1) * rows] = agg.T
    for copy in weights:
        copy.wait()
    both_w = jnp.concatenate([wn[...], ws[...]], axis=0)
    pair = 2
    span = pair * rows
    for i in range(blocks // pair):
        at = pl.ds(i * span, span)
        nodes_feat = table[pl.ds(i * pair, pair)].reshape(span, width)
        both = jnp.concatenate(
            [jnp.concatenate(aggs[i * pair : (i + 1) * pair], axis=0), nodes_feat], axis=1
        )
        value, slope = gate_of(dot(both, both_w))
        slope1[at] = slope
        hidden = value.astype(BF16)
        own2[pl.ds(i * pair, pair)] = hidden.reshape(pair, rows, width)
        hidden_t[:, at] = hidden.T
    out = pltpu.make_async_copy(own2, hidden_out, out_sem)
    out.start()
    out.wait()


def second_kernel(dims, *refs):
    peers, slots, blocks, picks, rows, width, bins_count, pay_rows = dims
    inc = peers - 1
    hbm_in, refs = refs[:7], refs[7:]
    (own2, slope1, tiles, tiles_t, agg1_t, feat_t, hidden_t), refs = refs[:7], refs[7:]
    past_in, refs = refs[:inc], refs[inc:]
    (grad_hidden_out, keep, send, back), refs = refs[:4], refs[4:]
    loaded, refs = refs[:7], refs[7:]
    table, agg_t, gtab, grad_hidden, pay, sems, out_sem = refs
    sources, wn, ws, hw, bins, flags, aux = loaded
    g = lax.axis_index("grp")
    core = lax.axis_index("clus") % CORES
    device = lax.axis_index("clus") * peers + g
    nodes = blocks * rows
    scale = 1.0 / (nodes * peers)
    loads = [
        pltpu.make_async_copy(src, dst, sems.at[i])
        for i, (src, dst) in enumerate(zip(hbm_in, loaded))
    ]
    for load in loads:
        load.start()
    table[pl.ds(0, blocks)] = own2[...]
    for step in range(1, peers):
        _, origin = partner(g, step, peers)
        table[pl.ds(blocks + origin * slots, slots)] = past_in[step - 1][...]
    back[...] = jnp.zeros(back.shape, F32)
    loads[0].wait()
    aggs = []
    for b in range(blocks):
        row = jnp.concatenate([tiles[b, k] for k in range(picks)], axis=1)
        agg = dot(row, gathered(table, sources, b, picks)).astype(BF16)
        aggs.append(agg)
        agg_t[:, b * rows : (b + 1) * rows] = agg.T
    for load in loads[1:]:
        load.wait()
    pair = 2
    span = pair * rows
    head = hw[...]
    step_col = lax.broadcasted_iota(jnp.int32, (bins_count, span), 0)
    both_w = jnp.concatenate([wn[...], ws[...]], axis=0)
    loss = jnp.zeros((bins_count, span), F32)
    ghw = jnp.zeros((bins_count, width), F32)
    grad_pres, grad_aggs = [], []
    for i in range(blocks // pair):
        at = pl.ds(i * pair, pair)
        both = jnp.concatenate(
            [
                jnp.concatenate(aggs[i * pair : (i + 1) * pair], axis=0),
                table[at].reshape(span, width),
            ],
            axis=1,
        )
        value, slope = gate_of(dot(both, both_w))
        hidden = value.astype(BF16)
        logits = dot_by_transpose(head, hidden)
        counted = step_col <= bins[i]
        event = jnp.where(step_col == bins[i], flags[i].astype(F32), 0.0)
        tail = jnp.exp(-jnp.abs(logits))
        soft = jnp.maximum(logits, 0.0) + jnp.log1p(tail)
        loss = loss + jnp.where(counted, soft, 0.0) - event * logits
        chance = jnp.where(logits >= 0.0, 1.0, tail) / (1.0 + tail)
        glog = (jnp.where(counted, chance, 0.0) - event).astype(BF16)
        ghw = ghw + dot(glog, hidden)
        grad_pre = (transpose_dot(glog, head) * slope).astype(BF16)
        grad_pres.append(grad_pre)
        grad_aggs.append(dot_by_transpose(grad_pre, wn[...]).astype(BF16))
        own = dot_by_transpose(grad_pre, ws[...]) + aux[at].reshape(span, width).astype(F32)
        gtab[at] = own.reshape(pair, rows, width)
    remote = pl.ds(blocks, peers * slots)
    gtab[remote] = jnp.zeros((peers * slots, rows, width), F32)
    for b in range(blocks):
        part = grad_aggs[b // pair][(b % pair) * rows : (b % pair + 1) * rows]
        spread = dot(tiles_t[b], part)
        for k in range(picks):
            gtab[sources[k, b]] += spread[k * rows : (k + 1) * rows]
    back[...] = gtab[remote]
    total = gtab[pl.ds(0, blocks)]
    grad_hidden[...] = total.astype(BF16)
    out = pltpu.make_async_copy(grad_hidden, grad_hidden_out, out_sem)
    out.start()
    grad_first = (total.reshape(nodes, width) * slope1[...]).astype(BF16)
    grad_second = jnp.concatenate(grad_pres, axis=0)
    terms = (
        (agg1_t, grad_first),
        (feat_t, grad_first),
        (agg_t, grad_second),
        (hidden_t, grad_second),
    )
    for n, (left, grads) in enumerate(terms):
        pay[pl.ds(n * width, width)] = (dot(left[...], grads) * scale).astype(BF16)
    part = jnp.sum(loss) * scale
    high = part.astype(BF16).astype(F32)
    tail_rows = pay_rows - 4 * width - bins_count
    lane = lax.broadcasted_iota(jnp.int32, (tail_rows, width), 0) * width + lax.broadcasted_iota(
        jnp.int32, (tail_rows, width), 1
    )
    loss_rows = jnp.where(lane == 2 * device, high, 0.0) + jnp.where(
        lane == 2 * device + 1, part - high, 0.0
    )
    pay[pl.ds(4 * width, bins_count)] = (ghw * scale).astype(BF16)
    pay[pl.ds(4 * width + bins_count, tail_rows)] = loss_rows.astype(BF16)
    half = pay_rows // CORES
    keep[...] = pay[pl.ds(pl.multiple_of(core * half, 16), half)]
    send[...] = pay[pl.ds(pl.multiple_of((1 - core) * half, 16), half)]
    out.wait()


def split_kernel(peers, kept, came, own, *outs):
    g = lax.axis_index("grp")

    def chunk(p):
        return (kept[p].astype(F32) + came[p].astype(F32)).astype(BF16)

    own[...] = chunk(g)
    for step in range(1, peers):
        peer, _ = partner(g, step, peers)
        outs[step - 1][...] = chunk(peer)


def add_kernel(*refs):
    total = refs[0][...].astype(F32)
    for ref in refs[1:-1]:
        if ref.shape == total.shape:
            total = total + ref[...].astype(F32)
    refs[-1][...] = total.astype(BF16)


def join_kernel(peers, own, *refs):
    out = refs[-1]
    g = lax.axis_index("grp")
    out[g] = own[...]
    for step in range(1, peers):
        _, origin = partner(g, step, peers)
        out[origin] = refs[step - 1][...]


def finish_kernel(dims, mine, other, *outs):
    width, bins_count, pay_rows = dims
    pay = outs[-1]
    half = pay_rows // CORES
    core = lax.axis_index("clus") % CORES
    pay[pl.ds(pl.multiple_of(core * half, 16), half)] = mine[...]
    pay[pl.ds(pl.multiple_of((1 - core) * half, 16), half)] = other[...]
    for i in range(4):
        outs[i][...] = pay[pl.ds(i * width, width)].astype(F32)
    outs[4][...] = pay[pl.ds(4 * width, bins_count)].astype(F32)
    loss_rows = pay[pl.ds(4 * width + bins_count, pay_rows - 4 * width - bins_count)].astype(F32)
    outs[5][0, 0] = jnp.sum(loss_rows)


def back_kernel(peers, slots, blocks, back, after, *outs):
    g = lax.axis_index("grp")
    for step in range(1, peers):
        _, origin = partner(g, step, peers)
        outs[step - 1][...] = back[pl.ds(origin * slots, slots)].astype(BF16)


def aux_kernel(peers, slots, blocks, send, *refs):
    back, out, token, total, lists, sem = refs[:-5], *refs[-5:]
    g = lax.axis_index("grp")
    listed = pltpu.make_async_copy(send, lists, sem)
    listed.start()
    total[...] = jnp.zeros_like(total)
    token[...] = jnp.zeros_like(token)
    listed.wait()
    for step in range(1, peers):
        peer, _ = partner(g, step, peers)
        for s in range(slots):
            total[lists[s, peer]] += back[step - 1][s].astype(F32)
    out[...] = total[pl.ds(0, blocks)].astype(BF16)


def shards(
    clus_count,
    peers,
    features,
    history,
    aux_history,
    tile_values,
    tile_sources,
    send_list,
    event_bins,
    event_flags,
    neigh_first,
    self_first,
    neigh_second,
    self_second,
    hazard_weight,
):
    blocks, picks, rows = tile_values.shape[2:5]
    width = features.shape[3]
    slots = send_list.shape[3]
    bins_count = hazard_weight.shape[1]
    devices = clus_count * peers
    chips_z = clus_count // CORES
    inc = peers - 1
    used = 4 * width + bins_count + -(-2 * devices // width)
    pay_rows = -(-used // (16 * CORES * peers)) * 16 * CORES * peers
    half = pay_rows // CORES
    chunk = half // peers
    block_shape = (blocks, rows, width)
    slot_shape = (slots, rows, width)
    routing = send_list[0, 0].T
    feat = features.reshape(block_shape)
    past = history.reshape(block_shape)
    params = pltpu.CompilerParams(vmem_limit_bytes=20 << 20)
    small = pltpu.CompilerParams(vmem_limit_bytes=4 << 20)

    def shape(dims, dtype=BF16):
        return jax.ShapeDtypeStruct(dims, dtype)

    def grp_pairs(step):
        return [(i, partner(i, step, peers)[0]) for i in range(peers)]

    def over_grp(value, step):
        return lax.ppermute(value, "grp", grp_pairs(step))

    def over_z(value, step):
        pairs = [
            (z * CORES + c, partner(z, step, chips_z)[0] * CORES + c)
            for z in range(chips_z)
            for c in range(CORES)
        ]
        return lax.ppermute(value, "clus", pairs)

    def over_core(value):
        return lax.ppermute(value, "clus", [(i, i ^ 1) for i in range(clus_count)])

    lists = (slots, peers)
    nodes = blocks * rows
    table = blocks + peers * slots
    tiles = tile_values[0, 0]
    sources = tile_sources[0, 0].T
    square = (width, width)
    turned = (width, nodes)
    packed = pl.pallas_call(
        functools.partial(pack_kernel, peers, slots, blocks),
        out_shape=[shape(slot_shape)] * (2 * inc) + [shape((8, 128), F32)],
        in_specs=[HBM] * 3,
        out_specs=[VMEM] * (2 * inc + 1),
        scratch_shapes=[
            pltpu.SMEM(lists, jnp.int32),
            pltpu.VMEM(block_shape, BF16),
            pltpu.VMEM(block_shape, BF16),
            pltpu.SemaphoreType.DMA((3,)),
        ],
        compiler_params=pltpu.CompilerParams(vmem_limit_bytes=PACK_LIMIT),
        name="pack",
    )(routing, feat, past)
    feat_in = [over_grp(packed[i], i + 1) for i in range(inc)]
    past_in = [over_grp(packed[inc + i], i + 1) for i in range(inc)]
    tiles, tiles_t, feat, feat_t = pl.pallas_call(
        functools.partial(prepare_kernel, (blocks, picks, rows)),
        out_shape=[
            shape(tiles.shape),
            shape((blocks, picks * rows, rows)),
            shape(block_shape),
            shape(turned),
        ],
        in_specs=[HBM] * 2 + [VMEM],
        out_specs=[VMEM] * 4,
        scratch_shapes=[pltpu.SemaphoreType.DMA((1 + blocks,))],
        compiler_params=pltpu.CompilerParams(vmem_limit_bytes=PREP_LIMIT),
        cost_estimate=pl.CostEstimate(flops=10**9, bytes_accessed=10**7, transcendentals=0),
        name="prepare",
    )(feat, tiles, packed[2 * inc])

    pair_shape = (blocks // 2, 1, 2 * rows)
    first = pl.pallas_call(
        functools.partial(first_kernel, (peers, slots, blocks, picks, rows, width)),
        out_shape=[
            shape(block_shape),
            shape(block_shape),
            shape((nodes, width), F32),
            shape(turned),
            shape(turned),
        ],
        in_specs=[HBM] * 3 + [VMEM] * (2 + inc),
        out_specs=[HBM] + [VMEM] * 4,
        scratch_shapes=[
            pltpu.VMEM((table, rows, width), BF16),
            pltpu.SMEM((picks, blocks), jnp.int32),
            pltpu.VMEM(square, BF16),
            pltpu.VMEM(square, BF16),
            pltpu.SemaphoreType.DMA((3,)),
            pltpu.SemaphoreType.DMA,
        ],
        compiler_params=params,
        name="first_layer",
    )(sources, neigh_first, self_first, feat, tiles, *feat_in)
    hidden_first = first[0]
    grad_hidden, kept, sent, gtab_back = pl.pallas_call(
        functools.partial(
            second_kernel, (peers, slots, blocks, picks, rows, width, bins_count, pay_rows)
        ),
        out_shape=[
            shape(block_shape),
            shape((half, width)),
            shape((half, width)),
            shape((peers * slots, rows, width), F32),
        ],
        in_specs=[HBM] * 7 + [VMEM] * (7 + inc),
        out_specs=[HBM] + [VMEM] * 3,
        scratch_shapes=[
            pltpu.SMEM((picks, blocks), jnp.int32),
            pltpu.VMEM(square, BF16),
            pltpu.VMEM(square, BF16),
            pltpu.VMEM((bins_count, width), BF16),
            pltpu.VMEM(pair_shape, jnp.int32),
            pltpu.VMEM(pair_shape, jnp.int32),
            pltpu.VMEM(block_shape, BF16),
            pltpu.VMEM((table, rows, width), BF16),
            pltpu.VMEM(turned, BF16),
            pltpu.VMEM((table, rows, width), F32),
            pltpu.VMEM(block_shape, BF16),
            pltpu.VMEM((pay_rows, width), BF16),
            pltpu.SemaphoreType.DMA((7,)),
            pltpu.SemaphoreType.DMA,
        ],
        compiler_params=params,
        name="second_layer",
    )(
        sources,
        neigh_second,
        self_second,
        hazard_weight.T,
        event_bins.reshape(pair_shape),
        event_flags.reshape(pair_shape),
        aux_history.reshape(block_shape),
        first[1],
        first[2],
        tiles,
        tiles_t,
        first[3],
        feat_t,
        first[4],
        *past_in,
    )

    came = over_core(sent)
    parts = pl.pallas_call(
        functools.partial(split_kernel, peers),
        out_shape=[shape((chunk, width))] * peers,
        in_specs=[VMEM, VMEM],
        out_specs=[VMEM] * peers,
        compiler_params=small,
        name="split",
    )(kept.reshape(peers, chunk, width), came.reshape(peers, chunk, width))
    from_grp = [over_grp(parts[i], i) for i in range(1, peers)]

    def add(*values):
        return pl.pallas_call(
            add_kernel,
            out_shape=shape((chunk, width)),
            in_specs=[VMEM] * len(values),
            out_specs=VMEM,
            compiler_params=small,
            name="add",
        )(*values)

    mine = add(parts[0], *from_grp)
    back = pl.pallas_call(
        functools.partial(back_kernel, peers, slots, blocks),
        out_shape=[shape(slot_shape)] * inc,
        in_specs=[VMEM, VMEM],
        out_specs=[VMEM] * inc,
        compiler_params=small,
        name="back",
    )(gtab_back, parts[0])
    came_back = [over_grp(back[i], i + 1) for i in range(inc)]
    new_aux, token = pl.pallas_call(
        functools.partial(aux_kernel, peers, slots, blocks),
        out_shape=[shape(block_shape), shape((8, 128), F32)],
        in_specs=[HBM] + [VMEM] * inc,
        out_specs=[VMEM] * 2,
        scratch_shapes=[
            pltpu.VMEM((blocks + 1, rows, width), F32),
            pltpu.SMEM(lists, jnp.int32),
            pltpu.SemaphoreType.DMA,
        ],
        compiler_params=small,
        cost_estimate=pl.CostEstimate(flops=AUX_FLOPS, bytes_accessed=10**6, transcendentals=0),
        name="aux",
    )(routing, *came_back)
    mine = add(mine, *[over_z(mine, i) for i in range(1, chips_z)])
    others = [over_grp(mine, i) for i in range(1, peers)]
    joined = pl.pallas_call(
        functools.partial(join_kernel, peers),
        out_shape=shape((peers, chunk, width)),
        in_specs=[VMEM] * (peers + 1),
        out_specs=VMEM,
        compiler_params=small,
        name="join",
    )(mine, *others, token).reshape(half, width)
    other_half = over_core(joined)
    grads = pl.pallas_call(
        functools.partial(finish_kernel, (width, bins_count, pay_rows)),
        out_shape=[shape(square, F32)] * 4 + [shape((bins_count, width), F32), shape((1, 1), F32)],
        in_specs=[VMEM] * 2,
        out_specs=[VMEM] * 5 + [SMEM],
        scratch_shapes=[pltpu.VMEM((pay_rows, width), BF16)],
        compiler_params=small,
        name="finish",
    )(joined, other_half)
    return (
        hidden_first.reshape(features.shape),
        grad_hidden.reshape(features.shape),
        new_aux.reshape(features.shape),
        *grads[:4],
        grads[4].T,
        grads[5][0, 0],
    )


def solution(mesh):
    split = P("clus", "grp")
    whole = P()
    return jax.shard_map(
        functools.partial(shards, mesh.shape["clus"], mesh.shape["grp"]),
        mesh=mesh,
        in_specs=(split,) * 8 + (whole,) * 5,
        out_specs=(split,) * 3 + (whole,) * 6,
        check_vma=False,
    )
```

```python
import functools

import jax
import jax.numpy as jnp
from jax import lax
from jax.experimental import pallas as pl
from jax.experimental.pallas import tpu as pltpu
from jax.sharding import PartitionSpec as P

BF16 = jnp.bfloat16
F32 = jnp.float32
VMEM = pl.BlockSpec(memory_space=pltpu.VMEM)
SMEM = pl.BlockSpec(memory_space=pltpu.SMEM)
HBM = pl.BlockSpec(memory_space=pltpu.HBM)
CORES = 2
PACK_LIMIT = 53 << 20
PREP_LIMIT = 4 << 20
AUX_FLOPS = 10**6


def dot(former, latter):
    return jnp.dot(former, latter, preferred_element_type=F32)


def transpose_dot(former, latter):
    return lax.dot_general(former, latter, (((0,), (0,)), ((), ())), preferred_element_type=F32)


def dot_by_transpose(former, latter):
    return lax.dot_general(former, latter, (((1,), (1,)), ((), ())), preferred_element_type=F32)


def partner(index, step, count):
    if count & (count - 1) == 0:
        return index ^ step, index ^ step
    return (index + step) % count, (index + count - step) % count


def pack_kernel(peers, slots, blocks, send, feat_in, past_in, *refs):
    outs, (token, lists, feat, past, sems) = refs[:-5], refs[-5:]
    g = lax.axis_index("grp")
    pairs = ((send, lists), (feat_in, feat), (past_in, past))
    copies = [pltpu.make_async_copy(src, dst, sems.at[i]) for i, (src, dst) in enumerate(pairs)]
    for copy in copies:
        copy.start()
    token[...] = jnp.zeros_like(token)
    copies[0].wait()
    for which, values in enumerate((feat, past)):
        copies[1 + which].wait()
        for step in range(1, peers):
            peer, _ = partner(g, step, peers)
            for s in range(slots):
                block = jnp.minimum(lists[s, peer], blocks - 1)
                outs[which * (peers - 1) + step - 1][s] = values[block]


def prepare_kernel(dims, feat, tiles, wn, ws, token, tiles_t, feat_t, w_t):
    blocks, picks, rows, width = dims
    w_t[:, :width] = wn[...].T
    w_t[:, width:] = ws[...].T
    for b in range(blocks):
        feat_t[:, b * rows : (b + 1) * rows] = feat[b].T
    for b in range(blocks):
        for k in range(picks):
            tiles_t[b, k * rows : (k + 1) * rows] = tiles[b, k].T


def gathered(table, sources, b, picks):
    return jnp.concatenate([table[sources[k, b]] for k in range(picks)], axis=0)


def gate_of(pre):
    gate = 0.5 * jnp.tanh(0.5 * pre) + 0.5
    value = pre * gate
    return value, gate + value * (1.0 - gate)


def first_kernel(dims, sources_in, wn, ws, feat, tiles, *refs):
    peers, slots, blocks, picks, rows, width = dims
    inc = peers - 1
    feat_in, refs = refs[:inc], refs[inc:]
    own2, slope1, agg_t, hidden_t, table, sources, sem = refs
    g = lax.axis_index("grp")
    listed = pltpu.make_async_copy(sources_in, sources, sem)
    listed.start()
    table[pl.ds(0, blocks)] = feat[...]
    for step in range(1, peers):
        _, origin = partner(g, step, peers)
        table[pl.ds(blocks + origin * slots, slots)] = feat_in[step - 1][...]
    listed.wait()
    aggs = []
    for b in range(blocks):
        row = jnp.concatenate([tiles[b, k] for k in range(picks)], axis=1)
        agg = dot(row, gathered(table, sources, b, picks)).astype(BF16)
        aggs.append(agg)
        agg_t[:, b * rows : (b + 1) * rows] = agg.T
    both_w = jnp.concatenate([wn[...], ws[...]], axis=0)
    pair = 2
    span = pair * rows
    for i in range(blocks // pair):
        at = pl.ds(i * span, span)
        nodes_feat = table[pl.ds(i * pair, pair)].reshape(span, width)
        both = jnp.concatenate(
            [jnp.concatenate(aggs[i * pair : (i + 1) * pair], axis=0), nodes_feat], axis=1
        )
        value, slope = gate_of(dot(both, both_w))
        slope1[at] = slope
        hidden = value.astype(BF16)
        own2[pl.ds(i * pair, pair)] = hidden.reshape(pair, rows, width)
        hidden_t[:, at] = hidden.T


def second_kernel(dims, sources_in, *refs):
    peers, slots, blocks, picks, rows, width, bins_count, pay_rows = dims
    inc = peers - 1
    (wn, ws, w_t, head, bins, flags, aux), refs = refs[:7], refs[7:]
    (own2, slope1, tiles, tiles_t, agg1_t, feat_t, hidden_t), refs = refs[:7], refs[7:]
    past_in, refs = refs[:inc], refs[inc:]
    (grad_hidden, keep, send, back), refs = refs[:4], refs[4:]
    sources, table, agg_t, gtab, pay, sem = refs
    g = lax.axis_index("grp")
    core = lax.axis_index("clus") % CORES
    device = lax.axis_index("clus") * peers + g
    nodes = blocks * rows
    scale = 1.0 / (nodes * peers)
    listed = pltpu.make_async_copy(sources_in, sources, sem)
    listed.start()
    table[pl.ds(0, blocks)] = own2[...]
    for step in range(1, peers):
        _, origin = partner(g, step, peers)
        table[pl.ds(blocks + origin * slots, slots)] = past_in[step - 1][...]
    remote = pl.ds(blocks, peers * slots)
    gtab[remote] = jnp.zeros((peers * slots, rows, width), F32)
    listed.wait()
    aggs = []
    for b in range(blocks):
        row = jnp.concatenate([tiles[b, k] for k in range(picks)], axis=1)
        agg = dot(row, gathered(table, sources, b, picks)).astype(BF16)
        aggs.append(agg)
        agg_t[:, b * rows : (b + 1) * rows] = agg.T
    pair = 2
    span = pair * rows
    step_col = lax.broadcasted_iota(jnp.int32, (bins_count, span), 0)
    both_w = jnp.concatenate([wn[...], ws[...]], axis=0)
    loss = jnp.zeros((bins_count, span), F32)
    ghw = jnp.zeros((bins_count, width), F32)
    chunks = range(blocks // pair)
    at = [pl.ds(i * pair, pair) for i in chunks]
    gates = []
    for i in chunks:
        both = jnp.concatenate(
            [
                jnp.concatenate(aggs[i * pair : (i + 1) * pair], axis=0),
                table[at[i]].reshape(span, width),
            ],
            axis=1,
        )
        gates.append(gate_of(dot(both, both_w)))
    hidden = [value.astype(BF16) for value, _ in gates]
    logits = [dot_by_transpose(head[...], hidden[i]) for i in chunks]
    glogs = []
    for i in chunks:
        counted = step_col <= bins[i]
        event = jnp.where(step_col == bins[i], flags[i].astype(F32), 0.0)
        tail = jnp.exp(-jnp.abs(logits[i]))
        soft = jnp.maximum(logits[i], 0.0) + jnp.log1p(tail)
        loss = loss + jnp.where(counted, soft, 0.0) - event * logits[i]
        chance = jnp.where(logits[i] >= 0.0, 1.0, tail) / (1.0 + tail)
        glogs.append((jnp.where(counted, chance, 0.0) - event).astype(BF16))
    grad_pres = [(transpose_dot(glogs[i], head[...]) * gates[i][1]).astype(BF16) for i in chunks]
    grad_aggs = []
    for i in chunks:
        onward = dot(grad_pres[i], w_t[...])
        grad_aggs.append(onward[:, :width].astype(BF16))
        own = onward[:, width:] + aux[at[i]].reshape(span, width).astype(F32)
        gtab[at[i]] = own.reshape(pair, rows, width)
    for i in chunks:
        ghw = ghw + dot(glogs[i], hidden[i])
    for b in range(blocks):
        part = grad_aggs[b // pair][(b % pair) * rows : (b % pair + 1) * rows]
        spread = dot(tiles_t[b], part)
        for k in range(picks):
            gtab[sources[k, b]] += spread[k * rows : (k + 1) * rows]
    back[...] = gtab[remote].astype(BF16)
    total = gtab[pl.ds(0, blocks)]
    grad_hidden[...] = total.astype(BF16)
    grad_first = (total.reshape(nodes, width) * slope1[...]).astype(BF16)
    grad_second = jnp.concatenate(grad_pres, axis=0)
    terms = (
        (agg1_t, grad_first),
        (feat_t, grad_first),
        (agg_t, grad_second),
        (hidden_t, grad_second),
    )
    for n, (left, grads) in enumerate(terms):
        pay[pl.ds(n * width, width)] = (dot(left[...], grads) * scale).astype(BF16)
    part = jnp.sum(loss) * scale
    high = part.astype(BF16).astype(F32)
    tail_rows = pay_rows - 4 * width - bins_count
    lane = lax.broadcasted_iota(jnp.int32, (tail_rows, width), 0) * width + lax.broadcasted_iota(
        jnp.int32, (tail_rows, width), 1
    )
    loss_rows = jnp.where(lane == 2 * device, high, 0.0) + jnp.where(
        lane == 2 * device + 1, part - high, 0.0
    )
    pay[pl.ds(4 * width, bins_count)] = (ghw * scale).astype(BF16)
    pay[pl.ds(4 * width + bins_count, tail_rows)] = loss_rows.astype(BF16)
    half = pay_rows // CORES
    keep[...] = pay[pl.ds(pl.multiple_of(core * half, 16), half)]
    send[...] = pay[pl.ds(pl.multiple_of((1 - core) * half, 16), half)]


def split_kernel(peers, kept, came, own, *outs):
    g = lax.axis_index("grp")

    def chunk(p):
        return (kept[p].astype(F32) + came[p].astype(F32)).astype(BF16)

    own[...] = chunk(g)
    for step in range(1, peers):
        peer, _ = partner(g, step, peers)
        outs[step - 1][...] = chunk(peer)


def store_kernel(hidden, grad_hidden, after, hidden_out, grad_hidden_out, token, sems):
    copies = [
        pltpu.make_async_copy(hidden, hidden_out, sems.at[0]),
        pltpu.make_async_copy(grad_hidden, grad_hidden_out, sems.at[1]),
    ]
    for copy in copies:
        copy.start()
    token[...] = jnp.zeros_like(token)
    for copy in copies:
        copy.wait()


def add_kernel(*refs):
    total = refs[0][...].astype(F32)
    for ref in refs[1:-1]:
        if ref.shape == total.shape:
            total = total + ref[...].astype(F32)
    refs[-1][...] = total.astype(BF16)


def join_kernel(peers, own, *refs):
    out = refs[-1]
    g = lax.axis_index("grp")
    out[g] = own[...]
    for step in range(1, peers):
        _, origin = partner(g, step, peers)
        out[origin] = refs[step - 1][...]


def finish_kernel(dims, mine, other, *outs):
    width, bins_count, pay_rows = dims
    pay = outs[-1]
    half = pay_rows // CORES
    core = lax.axis_index("clus") % CORES
    pay[pl.ds(pl.multiple_of(core * half, 16), half)] = mine[...]
    pay[pl.ds(pl.multiple_of((1 - core) * half, 16), half)] = other[...]
    for i in range(4):
        outs[i][...] = pay[pl.ds(i * width, width)].astype(F32)
    outs[4][...] = pay[pl.ds(4 * width, bins_count)].astype(F32)
    loss_rows = pay[pl.ds(4 * width + bins_count, pay_rows - 4 * width - bins_count)].astype(F32)
    outs[5][0, 0] = jnp.sum(loss_rows)


def back_kernel(peers, slots, blocks, back, after, *outs):
    g = lax.axis_index("grp")
    for step in range(1, peers):
        _, origin = partner(g, step, peers)
        outs[step - 1][...] = back[pl.ds(origin * slots, slots)]


def aux_kernel(peers, slots, blocks, send, *refs):
    back, out, token, total, lists, sem = refs[:-5], *refs[-5:]
    g = lax.axis_index("grp")
    listed = pltpu.make_async_copy(send, lists, sem)
    listed.start()
    total[...] = jnp.zeros_like(total)
    token[...] = jnp.zeros_like(token)
    listed.wait()
    for step in range(1, peers):
        peer, _ = partner(g, step, peers)
        for s in range(slots):
            total[lists[s, peer]] += back[step - 1][s].astype(F32)
    out[...] = total[pl.ds(0, blocks)].astype(BF16)


def shards(
    clus_count,
    peers,
    features,
    history,
    aux_history,
    tile_values,
    tile_sources,
    send_list,
    event_bins,
    event_flags,
    neigh_first,
    self_first,
    neigh_second,
    self_second,
    hazard_weight,
):
    blocks, picks, rows = tile_values.shape[2:5]
    width = features.shape[3]
    slots = send_list.shape[3]
    bins_count = hazard_weight.shape[1]
    devices = clus_count * peers
    chips_z = clus_count // CORES
    inc = peers - 1
    used = 4 * width + bins_count + -(-2 * devices // width)
    pay_rows = -(-used // (16 * CORES * peers)) * 16 * CORES * peers
    half = pay_rows // CORES
    chunk = half // peers
    block_shape = (blocks, rows, width)
    slot_shape = (slots, rows, width)
    routing = send_list[0, 0].T
    feat = features.reshape(block_shape)
    past = history.reshape(block_shape)
    params = pltpu.CompilerParams(vmem_limit_bytes=20 << 20)
    small = pltpu.CompilerParams(vmem_limit_bytes=4 << 20)

    def shape(dims, dtype=BF16):
        return jax.ShapeDtypeStruct(dims, dtype)

    def grp_pairs(step):
        return [(i, partner(i, step, peers)[0]) for i in range(peers)]

    def over_grp(value, step):
        return lax.ppermute(value, "grp", grp_pairs(step))

    def over_z(value, step):
        pairs = [
            (z * CORES + c, partner(z, step, chips_z)[0] * CORES + c)
            for z in range(chips_z)
            for c in range(CORES)
        ]
        return lax.ppermute(value, "clus", pairs)

    def over_core(value):
        return lax.ppermute(value, "clus", [(i, i ^ 1) for i in range(clus_count)])

    lists = (slots, peers)
    nodes = blocks * rows
    table = blocks + peers * slots
    tiles = tile_values[0, 0]
    sources = tile_sources[0, 0].T
    square = (width, width)
    turned = (width, nodes)
    packed = pl.pallas_call(
        functools.partial(pack_kernel, peers, slots, blocks),
        out_shape=[shape(slot_shape)] * (2 * inc) + [shape((8, 128), F32)],
        in_specs=[HBM] * 3,
        out_specs=[VMEM] * (2 * inc + 1),
        scratch_shapes=[
            pltpu.SMEM(lists, jnp.int32),
            pltpu.VMEM(block_shape, BF16),
            pltpu.VMEM(block_shape, BF16),
            pltpu.SemaphoreType.DMA((3,)),
        ],
        compiler_params=pltpu.CompilerParams(vmem_limit_bytes=PACK_LIMIT),
        name="pack",
    )(routing, feat, past)
    feat_in = [over_grp(packed[i], i + 1) for i in range(inc)]
    past_in = [over_grp(packed[inc + i], i + 1) for i in range(inc)]
    tiles_t, feat_t, w_t = pl.pallas_call(
        functools.partial(prepare_kernel, (blocks, picks, rows, width)),
        out_shape=[
            shape((blocks, picks * rows, rows)),
            shape(turned),
            shape((width, 2 * width)),
        ],
        in_specs=[VMEM] * 5,
        out_specs=[VMEM] * 3,
        compiler_params=pltpu.CompilerParams(vmem_limit_bytes=PREP_LIMIT),
        cost_estimate=pl.CostEstimate(flops=10**9, bytes_accessed=10**7, transcendentals=0),
        name="prepare",
    )(feat, tiles, neigh_second, self_second, packed[2 * inc])

    pair_shape = (blocks // 2, 1, 2 * rows)
    own2, slope1, agg_t, hidden_t = pl.pallas_call(
        functools.partial(first_kernel, (peers, slots, blocks, picks, rows, width)),
        out_shape=[shape(block_shape), shape((nodes, width), F32), shape(turned), shape(turned)],
        in_specs=[HBM] + [VMEM] * (4 + inc),
        out_specs=[VMEM] * 4,
        scratch_shapes=[
            pltpu.VMEM((table, rows, width), BF16),
            pltpu.SMEM((picks, blocks), jnp.int32),
            pltpu.SemaphoreType.DMA,
        ],
        compiler_params=params,
        name="first_layer",
    )(sources, neigh_first, self_first, feat, tiles, *feat_in)
    grad_hidden, kept, sent, back = pl.pallas_call(
        functools.partial(
            second_kernel, (peers, slots, blocks, picks, rows, width, bins_count, pay_rows)
        ),
        out_shape=[
            shape(block_shape),
            shape((half, width)),
            shape((half, width)),
            shape((peers * slots, rows, width)),
        ],
        in_specs=[HBM] + [VMEM] * (14 + inc),
        out_specs=[VMEM] * 4,
        scratch_shapes=[
            pltpu.SMEM((picks, blocks), jnp.int32),
            pltpu.VMEM((table, rows, width), BF16),
            pltpu.VMEM(turned, BF16),
            pltpu.VMEM((table, rows, width), F32),
            pltpu.VMEM((pay_rows, width), BF16),
            pltpu.SemaphoreType.DMA,
        ],
        compiler_params=params,
        name="second_layer",
    )(
        sources,
        neigh_second,
        self_second,
        w_t,
        hazard_weight.T,
        event_bins.reshape(pair_shape),
        event_flags.reshape(pair_shape),
        aux_history.reshape(block_shape),
        own2,
        slope1,
        tiles,
        tiles_t,
        agg_t,
        feat_t,
        hidden_t,
        *past_in,
    )

    came = over_core(sent)
    parts = pl.pallas_call(
        functools.partial(split_kernel, peers),
        out_shape=[shape((chunk, width))] * peers,
        in_specs=[VMEM, VMEM],
        out_specs=[VMEM] * peers,
        compiler_params=small,
        name="split",
    )(kept.reshape(peers, chunk, width), came.reshape(peers, chunk, width))
    from_grp = [over_grp(parts[i], i) for i in range(1, peers)]

    def add(*values):
        return pl.pallas_call(
            add_kernel,
            out_shape=shape((chunk, width)),
            in_specs=[VMEM] * len(values),
            out_specs=VMEM,
            compiler_params=small,
            name="add",
        )(*values)

    hidden_first, grad_hidden, stored = pl.pallas_call(
        store_kernel,
        out_shape=[shape(block_shape), shape(block_shape), shape((8, 128), F32)],
        in_specs=[VMEM] * 3,
        out_specs=[HBM, HBM, VMEM],
        scratch_shapes=[pltpu.SemaphoreType.DMA((2,))],
        compiler_params=small,
        name="store",
    )(own2, grad_hidden, parts[0])
    mine = add(parts[0], *from_grp, stored)
    back = pl.pallas_call(
        functools.partial(back_kernel, peers, slots, blocks),
        out_shape=[shape(slot_shape)] * inc,
        in_specs=[VMEM, VMEM],
        out_specs=[VMEM] * inc,
        compiler_params=small,
        name="back",
    )(back, parts[0])
    came_back = [over_grp(back[i], i + 1) for i in range(inc)]
    new_aux, token = pl.pallas_call(
        functools.partial(aux_kernel, peers, slots, blocks),
        out_shape=[shape(block_shape), shape((8, 128), F32)],
        in_specs=[HBM] + [VMEM] * inc,
        out_specs=[VMEM] * 2,
        scratch_shapes=[
            pltpu.VMEM((blocks + 1, rows, width), F32),
            pltpu.SMEM(lists, jnp.int32),
            pltpu.SemaphoreType.DMA,
        ],
        compiler_params=small,
        cost_estimate=pl.CostEstimate(flops=AUX_FLOPS, bytes_accessed=10**6, transcendentals=0),
        name="aux",
    )(routing, *came_back)
    mine = add(mine, *[over_z(mine, i) for i in range(1, chips_z)])
    others = [over_grp(mine, i) for i in range(1, peers)]
    joined = pl.pallas_call(
        functools.partial(join_kernel, peers),
        out_shape=shape((peers, chunk, width)),
        in_specs=[VMEM] * (peers + 1),
        out_specs=VMEM,
        compiler_params=small,
        name="join",
    )(mine, *others, token).reshape(half, width)
    other_half = over_core(joined)
    grads = pl.pallas_call(
        functools.partial(finish_kernel, (width, bins_count, pay_rows)),
        out_shape=[shape(square, F32)] * 4 + [shape((bins_count, width), F32), shape((1, 1), F32)],
        in_specs=[VMEM] * 2,
        out_specs=[VMEM] * 5 + [SMEM],
        scratch_shapes=[pltpu.VMEM((pay_rows, width), BF16)],
        compiler_params=small,
        name="finish",
    )(joined, other_half)
    return (
        hidden_first.reshape(features.shape),
        grad_hidden.reshape(features.shape),
        new_aux.reshape(features.shape),
        *grads[:4],
        grads[4].T,
        grads[5][0, 0],
    )


def solution(mesh):
    split = P("clus", "grp")
    whole = P()
    return jax.shard_map(
        functools.partial(shards, mesh.shape["clus"], mesh.shape["grp"]),
        mesh=mesh,
        in_specs=(split,) * 8 + (whole,) * 5,
        out_specs=(split,) * 3 + (whole,) * 6,
        check_vma=False,
    )
```

```python
import functools

import jax
import jax.numpy as jnp
from jax import lax
from jax.experimental import pallas as pl
from jax.experimental.pallas import tpu as pltpu
from jax.sharding import PartitionSpec as P

BF16 = jnp.bfloat16
F32 = jnp.float32
VMEM = pl.BlockSpec(memory_space=pltpu.VMEM)
SMEM = pl.BlockSpec(memory_space=pltpu.SMEM)
HBM = pl.BlockSpec(memory_space=pltpu.HBM)
CORES = 2
PACK_LIMIT = 53 << 20
PREP_LIMIT = 4 << 20
AUX_FLOPS = 10**6


def dot(former, latter):
    return jnp.dot(former, latter, preferred_element_type=F32)


def transpose_dot(former, latter):
    return lax.dot_general(former, latter, (((0,), (0,)), ((), ())), preferred_element_type=F32)


def dot_by_transpose(former, latter):
    return lax.dot_general(former, latter, (((1,), (1,)), ((), ())), preferred_element_type=F32)


def partner(index, step, count):
    if count & (count - 1) == 0:
        return index ^ step, index ^ step
    return (index + step) % count, (index + count - step) % count


def pack_kernel(peers, slots, blocks, send, feat_in, past_in, *refs):
    outs, (token, lists, feat, past, sems) = refs[:-5], refs[-5:]
    g = lax.axis_index("grp")
    pairs = ((send, lists), (feat_in, feat), (past_in, past))
    copies = [pltpu.make_async_copy(src, dst, sems.at[i]) for i, (src, dst) in enumerate(pairs)]
    for copy in copies:
        copy.start()
    token[...] = jnp.zeros_like(token)
    copies[0].wait()
    for which, values in enumerate((feat, past)):
        copies[1 + which].wait()
        for step in range(1, peers):
            peer, _ = partner(g, step, peers)
            for s in range(slots):
                block = jnp.minimum(lists[s, peer], blocks - 1)
                outs[which * (peers - 1) + step - 1][s] = values[block]


def prepare_kernel(dims, feat, tiles, token, tiles_t, feat_t, feat_kept):
    blocks, picks, rows = dims
    feat_kept[...] = feat[...]
    for b in range(blocks):
        feat_t[:, b * rows : (b + 1) * rows] = feat[b].T
    for b in range(blocks):
        for k in range(picks):
            tiles_t[b, k * rows : (k + 1) * rows] = tiles[b, k].T


def gathered(table, sources, b, picks):
    return jnp.concatenate([table[sources[k, b]] for k in range(picks)], axis=0)


def gate_of(pre):
    gate = 0.5 * jnp.tanh(0.5 * pre) + 0.5
    value = pre * gate
    return value, gate + value * (1.0 - gate)


def first_kernel(dims, sources_in, wn, ws, wn_next, ws_next, head, bins, flags, feat, tiles, *refs):
    peers, slots, blocks, picks, rows, width = dims
    inc = peers - 1
    feat_in, refs = refs[:inc], refs[inc:]
    own2, slope1, agg_t, hidden_t, w, w_t, head_kept, bins_kept, flags_kept = refs[:9]
    table, sources, sem = refs[9:]
    g = lax.axis_index("grp")
    listed = pltpu.make_async_copy(sources_in, sources, sem)
    listed.start()
    table[pl.ds(0, blocks)] = feat[...]
    for step in range(1, peers):
        _, origin = partner(g, step, peers)
        table[pl.ds(blocks + origin * slots, slots)] = feat_in[step - 1][...]
    head_kept[...] = head[...]
    bins_kept[...] = bins[...]
    flags_kept[...] = flags[...]
    w[:width] = wn_next[...]
    w[width:] = ws_next[...]
    w_t[:, :width] = wn_next[...].T
    w_t[:, width:] = ws_next[...].T
    listed.wait()
    aggs = []
    for b in range(blocks):
        row = jnp.concatenate([tiles[b, k] for k in range(picks)], axis=1)
        agg = dot(row, gathered(table, sources, b, picks)).astype(BF16)
        aggs.append(agg)
        agg_t[:, b * rows : (b + 1) * rows] = agg.T
    both_w = jnp.concatenate([wn[...], ws[...]], axis=0)
    pair = 2
    span = pair * rows
    for i in range(blocks // pair):
        at = pl.ds(i * span, span)
        nodes_feat = table[pl.ds(i * pair, pair)].reshape(span, width)
        both = jnp.concatenate(
            [jnp.concatenate(aggs[i * pair : (i + 1) * pair], axis=0), nodes_feat], axis=1
        )
        value, slope = gate_of(dot(both, both_w))
        slope1[at] = slope
        hidden = value.astype(BF16)
        own2[pl.ds(i * pair, pair)] = hidden.reshape(pair, rows, width)
        hidden_t[:, at] = hidden.T


def second_kernel(dims, sources_in, *refs):
    peers, slots, blocks, picks, rows, width, bins_count, pay_rows = dims
    inc = peers - 1
    (w, w_t, head, bins, flags, aux), refs = refs[:6], refs[6:]
    (own2, slope1, tiles, tiles_t, agg1_t, feat_t, hidden_t), refs = refs[:7], refs[7:]
    past_in, refs = refs[:inc], refs[inc:]
    (grad_hidden, keep, send, back), refs = refs[:4], refs[4:]
    sources, table, agg_t, gtab, pay, sem = refs
    g = lax.axis_index("grp")
    core = lax.axis_index("clus") % CORES
    device = lax.axis_index("clus") * peers + g
    nodes = blocks * rows
    scale = 1.0 / (nodes * peers)
    listed = pltpu.make_async_copy(sources_in, sources, sem)
    listed.start()
    table[pl.ds(0, blocks)] = own2[...]
    for step in range(1, peers):
        _, origin = partner(g, step, peers)
        table[pl.ds(blocks + origin * slots, slots)] = past_in[step - 1][...]
    remote = pl.ds(blocks, peers * slots)
    gtab[remote] = jnp.zeros((peers * slots, rows, width), F32)
    listed.wait()
    aggs = []
    for b in range(blocks):
        row = jnp.concatenate([tiles[b, k] for k in range(picks)], axis=1)
        agg = dot(row, gathered(table, sources, b, picks)).astype(BF16)
        aggs.append(agg)
        agg_t[:, b * rows : (b + 1) * rows] = agg.T
    pair = 2
    span = pair * rows
    step_col = lax.broadcasted_iota(jnp.int32, (bins_count, span), 0)
    loss = jnp.zeros((bins_count, span), F32)
    ghw = jnp.zeros((bins_count, width), F32)
    chunks = range(blocks // pair)
    at = [pl.ds(i * pair, pair) for i in chunks]
    gates = []
    for i in chunks:
        both = jnp.concatenate(
            [
                jnp.concatenate(aggs[i * pair : (i + 1) * pair], axis=0),
                table[at[i]].reshape(span, width),
            ],
            axis=1,
        )
        gates.append(gate_of(dot(both, w[...])))
    hidden = [value.astype(BF16) for value, _ in gates]
    logits = [dot_by_transpose(head[...], hidden[i]) for i in chunks]
    glogs = []
    for i in chunks:
        counted = step_col <= bins[i]
        event = jnp.where(step_col == bins[i], flags[i].astype(F32), 0.0)
        tail = jnp.exp(-jnp.abs(logits[i]))
        soft = jnp.maximum(logits[i], 0.0) + jnp.log1p(tail)
        loss = loss + jnp.where(counted, soft, 0.0) - event * logits[i]
        chance = jnp.where(logits[i] >= 0.0, 1.0, tail) / (1.0 + tail)
        glogs.append((jnp.where(counted, chance, 0.0) - event).astype(BF16))
    grad_pres = [(transpose_dot(glogs[i], head[...]) * gates[i][1]).astype(BF16) for i in chunks]
    grad_aggs = []
    for i in chunks:
        onward = dot(grad_pres[i], w_t[...])
        grad_aggs.append(onward[:, :width].astype(BF16))
        own = onward[:, width:] + aux[at[i]].reshape(span, width).astype(F32)
        gtab[at[i]] = own.reshape(pair, rows, width)
    for i in chunks:
        ghw = ghw + dot(glogs[i], hidden[i])
    for b in range(blocks):
        part = grad_aggs[b // pair][(b % pair) * rows : (b % pair + 1) * rows]
        spread = dot(tiles_t[b], part)
        for k in range(picks):
            gtab[sources[k, b]] += spread[k * rows : (k + 1) * rows]
    back[...] = gtab[remote].astype(BF16)
    total = gtab[pl.ds(0, blocks)]
    grad_hidden[...] = total.astype(BF16)
    grad_first = (total.reshape(nodes, width) * slope1[...]).astype(BF16)
    grad_second = jnp.concatenate(grad_pres, axis=0)
    terms = (
        (agg1_t, grad_first),
        (feat_t, grad_first),
        (agg_t, grad_second),
        (hidden_t, grad_second),
    )
    for n, (left, grads) in enumerate(terms):
        pay[pl.ds(n * width, width)] = (dot(left[...], grads) * scale).astype(BF16)
    part = jnp.sum(loss) * scale
    high = part.astype(BF16).astype(F32)
    tail_rows = pay_rows - 4 * width - bins_count
    lane = lax.broadcasted_iota(jnp.int32, (tail_rows, width), 0) * width + lax.broadcasted_iota(
        jnp.int32, (tail_rows, width), 1
    )
    loss_rows = jnp.where(lane == 2 * device, high, 0.0) + jnp.where(
        lane == 2 * device + 1, part - high, 0.0
    )
    pay[pl.ds(4 * width, bins_count)] = (ghw * scale).astype(BF16)
    pay[pl.ds(4 * width + bins_count, tail_rows)] = loss_rows.astype(BF16)
    half = pay_rows // CORES
    keep[...] = pay[pl.ds(pl.multiple_of(core * half, 16), half)]
    send[...] = pay[pl.ds(pl.multiple_of((1 - core) * half, 16), half)]


def split_kernel(peers, kept, came, own, *outs):
    g = lax.axis_index("grp")

    def chunk(p):
        return (kept[p].astype(F32) + came[p].astype(F32)).astype(BF16)

    own[...] = chunk(g)
    for step in range(1, peers):
        peer, _ = partner(g, step, peers)
        outs[step - 1][...] = chunk(peer)


def store_kernel(hidden, grad_hidden, after, hidden_out, grad_hidden_out, token, sems):
    copies = [
        pltpu.make_async_copy(hidden, hidden_out, sems.at[0]),
        pltpu.make_async_copy(grad_hidden, grad_hidden_out, sems.at[1]),
    ]
    for copy in copies:
        copy.start()
    token[...] = jnp.zeros_like(token)
    for copy in copies:
        copy.wait()


def add_kernel(*refs):
    total = refs[0][...].astype(F32)
    for ref in refs[1:-1]:
        if ref.shape == total.shape:
            total = total + ref[...].astype(F32)
    refs[-1][...] = total.astype(BF16)


def join_kernel(peers, own, *refs):
    out = refs[-1]
    g = lax.axis_index("grp")
    out[g] = own[...]
    for step in range(1, peers):
        _, origin = partner(g, step, peers)
        out[origin] = refs[step - 1][...]


def finish_kernel(dims, mine, other, *outs):
    width, bins_count, pay_rows = dims
    pay = outs[-1]
    half = pay_rows // CORES
    core = lax.axis_index("clus") % CORES
    pay[pl.ds(pl.multiple_of(core * half, 16), half)] = mine[...]
    pay[pl.ds(pl.multiple_of((1 - core) * half, 16), half)] = other[...]
    for i in range(4):
        outs[i][...] = pay[pl.ds(i * width, width)].astype(F32)
    outs[4][...] = pay[pl.ds(4 * width, bins_count)].astype(F32)
    loss_rows = pay[pl.ds(4 * width + bins_count, pay_rows - 4 * width - bins_count)].astype(F32)
    outs[5][0, 0] = jnp.sum(loss_rows)


def back_kernel(peers, slots, blocks, back, after, *outs):
    g = lax.axis_index("grp")
    for step in range(1, peers):
        _, origin = partner(g, step, peers)
        outs[step - 1][...] = back[pl.ds(origin * slots, slots)]


def aux_kernel(peers, slots, blocks, send, *refs):
    back, out, token, total, lists, sem = refs[:-5], *refs[-5:]
    g = lax.axis_index("grp")
    listed = pltpu.make_async_copy(send, lists, sem)
    listed.start()
    total[...] = jnp.zeros_like(total)
    token[...] = jnp.zeros_like(token)
    listed.wait()
    for step in range(1, peers):
        peer, _ = partner(g, step, peers)
        for s in range(slots):
            total[lists[s, peer]] += back[step - 1][s].astype(F32)
    out[...] = total[pl.ds(0, blocks)].astype(BF16)


def shards(
    clus_count,
    peers,
    features,
    history,
    aux_history,
    tile_values,
    tile_sources,
    send_list,
    event_bins,
    event_flags,
    neigh_first,
    self_first,
    neigh_second,
    self_second,
    hazard_weight,
):
    blocks, picks, rows = tile_values.shape[2:5]
    width = features.shape[3]
    slots = send_list.shape[3]
    bins_count = hazard_weight.shape[1]
    devices = clus_count * peers
    chips_z = clus_count // CORES
    inc = peers - 1
    used = 4 * width + bins_count + -(-2 * devices // width)
    pay_rows = -(-used // (16 * CORES * peers)) * 16 * CORES * peers
    half = pay_rows // CORES
    chunk = half // peers
    block_shape = (blocks, rows, width)
    slot_shape = (slots, rows, width)
    routing = send_list[0, 0].T
    feat = features.reshape(block_shape)
    past = history.reshape(block_shape)
    params = pltpu.CompilerParams(vmem_limit_bytes=20 << 20)
    small = pltpu.CompilerParams(vmem_limit_bytes=4 << 20)

    def shape(dims, dtype=BF16):
        return jax.ShapeDtypeStruct(dims, dtype)

    def grp_pairs(step):
        return [(i, partner(i, step, peers)[0]) for i in range(peers)]

    def over_grp(value, step):
        return lax.ppermute(value, "grp", grp_pairs(step))

    def over_z(value, step):
        pairs = [
            (z * CORES + c, partner(z, step, chips_z)[0] * CORES + c)
            for z in range(chips_z)
            for c in range(CORES)
        ]
        return lax.ppermute(value, "clus", pairs)

    def over_core(value):
        return lax.ppermute(value, "clus", [(i, i ^ 1) for i in range(clus_count)])

    lists = (slots, peers)
    nodes = blocks * rows
    table = blocks + peers * slots
    tiles = tile_values[0, 0]
    sources = tile_sources[0, 0].T
    square = (width, width)
    turned = (width, nodes)
    packed = pl.pallas_call(
        functools.partial(pack_kernel, peers, slots, blocks),
        out_shape=[shape(slot_shape)] * (2 * inc) + [shape((8, 128), F32)],
        in_specs=[HBM] * 3,
        out_specs=[VMEM] * (2 * inc + 1),
        scratch_shapes=[
            pltpu.SMEM(lists, jnp.int32),
            pltpu.VMEM(block_shape, BF16),
            pltpu.VMEM(block_shape, BF16),
            pltpu.SemaphoreType.DMA((3,)),
        ],
        compiler_params=pltpu.CompilerParams(vmem_limit_bytes=PACK_LIMIT),
        name="pack",
    )(routing, feat, past)
    feat_in = [over_grp(packed[i], i + 1) for i in range(inc)]
    past_in = [over_grp(packed[inc + i], i + 1) for i in range(inc)]
    tiles_t, feat_t, feat = pl.pallas_call(
        functools.partial(prepare_kernel, (blocks, picks, rows)),
        out_shape=[
            shape((blocks, picks * rows, rows)),
            shape(turned),
            shape(block_shape),
        ],
        in_specs=[VMEM] * 3,
        out_specs=[VMEM] * 3,
        compiler_params=pltpu.CompilerParams(vmem_limit_bytes=PREP_LIMIT),
        cost_estimate=pl.CostEstimate(flops=10**9, bytes_accessed=10**7, transcendentals=0),
        name="prepare",
    )(feat, tiles, packed[2 * inc])

    pair_shape = (blocks // 2, 1, 2 * rows)
    own2, slope1, agg_t, hidden_t, w, w_t, head, bins, flags = pl.pallas_call(
        functools.partial(first_kernel, (peers, slots, blocks, picks, rows, width)),
        out_shape=[
            shape(block_shape),
            shape((nodes, width), F32),
            shape(turned),
            shape(turned),
            shape((2 * width, width)),
            shape((width, 2 * width)),
            shape((bins_count, width)),
            shape(pair_shape, jnp.int32),
            shape(pair_shape, jnp.int32),
        ],
        in_specs=[HBM] + [VMEM] * (9 + inc),
        out_specs=[VMEM] * 9,
        scratch_shapes=[
            pltpu.VMEM((table, rows, width), BF16),
            pltpu.SMEM((picks, blocks), jnp.int32),
            pltpu.SemaphoreType.DMA,
        ],
        compiler_params=params,
        name="first_layer",
    )(
        sources,
        neigh_first,
        self_first,
        neigh_second,
        self_second,
        hazard_weight.T,
        event_bins.reshape(pair_shape),
        event_flags.reshape(pair_shape),
        feat,
        tiles,
        *feat_in,
    )
    grad_hidden, kept, sent, back = pl.pallas_call(
        functools.partial(
            second_kernel, (peers, slots, blocks, picks, rows, width, bins_count, pay_rows)
        ),
        out_shape=[
            shape(block_shape),
            shape((half, width)),
            shape((half, width)),
            shape((peers * slots, rows, width)),
        ],
        in_specs=[HBM] + [VMEM] * (13 + inc),
        out_specs=[VMEM] * 4,
        scratch_shapes=[
            pltpu.SMEM((picks, blocks), jnp.int32),
            pltpu.VMEM((table, rows, width), BF16),
            pltpu.VMEM(turned, BF16),
            pltpu.VMEM((table, rows, width), F32),
            pltpu.VMEM((pay_rows, width), BF16),
            pltpu.SemaphoreType.DMA,
        ],
        compiler_params=params,
        name="second_layer",
    )(
        sources,
        w,
        w_t,
        head,
        bins,
        flags,
        aux_history.reshape(block_shape),
        own2,
        slope1,
        tiles,
        tiles_t,
        agg_t,
        feat_t,
        hidden_t,
        *past_in,
    )

    came = over_core(sent)
    parts = pl.pallas_call(
        functools.partial(split_kernel, peers),
        out_shape=[shape((chunk, width))] * peers,
        in_specs=[VMEM, VMEM],
        out_specs=[VMEM] * peers,
        compiler_params=small,
        name="split",
    )(kept.reshape(peers, chunk, width), came.reshape(peers, chunk, width))
    from_grp = [over_grp(parts[i], i) for i in range(1, peers)]

    def add(*values):
        return pl.pallas_call(
            add_kernel,
            out_shape=shape((chunk, width)),
            in_specs=[VMEM] * len(values),
            out_specs=VMEM,
            compiler_params=small,
            name="add",
        )(*values)

    hidden_first, grad_hidden, stored = pl.pallas_call(
        store_kernel,
        out_shape=[shape(block_shape), shape(block_shape), shape((8, 128), F32)],
        in_specs=[VMEM] * 3,
        out_specs=[HBM, HBM, VMEM],
        scratch_shapes=[pltpu.SemaphoreType.DMA((2,))],
        compiler_params=small,
        name="store",
    )(own2, grad_hidden, parts[0])
    mine = add(parts[0], *from_grp, stored)
    back = pl.pallas_call(
        functools.partial(back_kernel, peers, slots, blocks),
        out_shape=[shape(slot_shape)] * inc,
        in_specs=[VMEM, VMEM],
        out_specs=[VMEM] * inc,
        compiler_params=small,
        name="back",
    )(back, parts[0])
    came_back = [over_grp(back[i], i + 1) for i in range(inc)]
    new_aux, token = pl.pallas_call(
        functools.partial(aux_kernel, peers, slots, blocks),
        out_shape=[shape(block_shape), shape((8, 128), F32)],
        in_specs=[HBM] + [VMEM] * inc,
        out_specs=[VMEM] * 2,
        scratch_shapes=[
            pltpu.VMEM((blocks + 1, rows, width), F32),
            pltpu.SMEM(lists, jnp.int32),
            pltpu.SemaphoreType.DMA,
        ],
        compiler_params=small,
        cost_estimate=pl.CostEstimate(flops=AUX_FLOPS, bytes_accessed=10**6, transcendentals=0),
        name="aux",
    )(routing, *came_back)
    mine = add(mine, *[over_z(mine, i) for i in range(1, chips_z)])
    others = [over_grp(mine, i) for i in range(1, peers)]
    joined = pl.pallas_call(
        functools.partial(join_kernel, peers),
        out_shape=shape((peers, chunk, width)),
        in_specs=[VMEM] * (peers + 1),
        out_specs=VMEM,
        compiler_params=small,
        name="join",
    )(mine, *others, token).reshape(half, width)
    other_half = over_core(joined)
    grads = pl.pallas_call(
        functools.partial(finish_kernel, (width, bins_count, pay_rows)),
        out_shape=[shape(square, F32)] * 4 + [shape((bins_count, width), F32), shape((1, 1), F32)],
        in_specs=[VMEM] * 2,
        out_specs=[VMEM] * 5 + [SMEM],
        scratch_shapes=[pltpu.VMEM((pay_rows, width), BF16)],
        compiler_params=small,
        name="finish",
    )(joined, other_half)
    return (
        hidden_first.reshape(features.shape),
        grad_hidden.reshape(features.shape),
        new_aux.reshape(features.shape),
        *grads[:4],
        grads[4].T,
        grads[5][0, 0],
    )


def solution(mesh):
    split = P("clus", "grp")
    whole = P()
    return jax.shard_map(
        functools.partial(shards, mesh.shape["clus"], mesh.shape["grp"]),
        mesh=mesh,
        in_specs=(split,) * 8 + (whole,) * 5,
        out_specs=(split,) * 3 + (whole,) * 6,
        check_vma=False,
    )
```

```python
import functools

import jax
import jax.numpy as jnp
from jax import lax
from jax.experimental import pallas as pl
from jax.experimental.pallas import tpu as pltpu
from jax.sharding import PartitionSpec as P

BF16 = jnp.bfloat16
F32 = jnp.float32
VMEM = pl.BlockSpec(memory_space=pltpu.VMEM)
SMEM = pl.BlockSpec(memory_space=pltpu.SMEM)
HBM = pl.BlockSpec(memory_space=pltpu.HBM)
CORES = 2
PACK_LIMIT = 53 << 20
PREP_LIMIT = 4 << 20
AUX_FLOPS = 10**6


def dot(former, latter):
    return jnp.dot(former, latter, preferred_element_type=F32)


def transpose_dot(former, latter):
    return lax.dot_general(former, latter, (((0,), (0,)), ((), ())), preferred_element_type=F32)


def dot_by_transpose(former, latter):
    return lax.dot_general(former, latter, (((1,), (1,)), ((), ())), preferred_element_type=F32)


def partner(index, step, count):
    if count & (count - 1) == 0:
        return index ^ step, index ^ step
    return (index + step) % count, (index + count - step) % count


def pack_kernel(peers, slots, blocks, send, feat_in, past_in, *refs):
    outs, (token, lists, feat, past, sems) = refs[:-5], refs[-5:]
    g = lax.axis_index("grp")
    pairs = ((send, lists), (feat_in, feat), (past_in, past))
    copies = [pltpu.make_async_copy(src, dst, sems.at[i]) for i, (src, dst) in enumerate(pairs)]
    for copy in copies:
        copy.start()
    token[...] = jnp.zeros_like(token)
    copies[0].wait()
    for which, values in enumerate((feat, past)):
        copies[1 + which].wait()
        for step in range(1, peers):
            peer, _ = partner(g, step, peers)
            for s in range(slots):
                block = jnp.minimum(lists[s, peer], blocks - 1)
                outs[which * (peers - 1) + step - 1][s] = values[block]


def prepare_kernel(dims, feat, tiles, token, tiles_t, feat_t, feat_kept):
    blocks, picks, rows = dims
    feat_kept[...] = feat[...]
    for b in range(blocks):
        feat_t[:, b * rows : (b + 1) * rows] = feat[b].T
    for b in range(blocks):
        for k in range(picks):
            tiles_t[b, k * rows : (k + 1) * rows] = tiles[b, k].T


def gathered(table, sources, b, picks):
    return jnp.concatenate([table[sources[k, b]] for k in range(picks)], axis=0)


def gate_of(pre):
    gate = 0.5 * jnp.tanh(0.5 * pre) + 0.5
    value = pre * gate
    return value, gate + value * (1.0 - gate)


def first_kernel(dims, sources_in, wn, ws, wn_next, ws_next, head, bins, flags, feat, tiles, *refs):
    peers, slots, blocks, picks, rows, width = dims
    inc = peers - 1
    feat_in, refs = refs[:inc], refs[inc:]
    own2, slope1, agg_t, hidden_t, self2, w, w_t, head_kept, bins_kept, flags_kept = refs[:10]
    table, sources, sem = refs[10:]
    g = lax.axis_index("grp")
    listed = pltpu.make_async_copy(sources_in, sources, sem)
    listed.start()
    table[pl.ds(0, blocks)] = feat[...]
    for step in range(1, peers):
        _, origin = partner(g, step, peers)
        table[pl.ds(blocks + origin * slots, slots)] = feat_in[step - 1][...]
    head_kept[...] = head[...]
    bins_kept[...] = bins[...]
    flags_kept[...] = flags[...]
    w[...] = wn_next[...]
    w_t[:, :width] = wn_next[...].T
    w_t[:, width:] = ws_next[...].T
    listed.wait()
    aggs = []
    for b in range(blocks):
        row = jnp.concatenate([tiles[b, k] for k in range(picks)], axis=1)
        agg = dot(row, gathered(table, sources, b, picks)).astype(BF16)
        aggs.append(agg)
        agg_t[:, b * rows : (b + 1) * rows] = agg.T
    both_w = jnp.concatenate([wn[...], ws[...]], axis=0)
    pair = 2
    span = pair * rows
    for i in range(blocks // pair):
        at = pl.ds(i * span, span)
        nodes_feat = table[pl.ds(i * pair, pair)].reshape(span, width)
        both = jnp.concatenate(
            [jnp.concatenate(aggs[i * pair : (i + 1) * pair], axis=0), nodes_feat], axis=1
        )
        value, slope = gate_of(dot(both, both_w))
        slope1[at] = slope
        hidden = value.astype(BF16)
        own2[pl.ds(i * pair, pair)] = hidden.reshape(pair, rows, width)
        hidden_t[:, at] = hidden.T
        self2[at] = dot(hidden, ws_next[...])


def second_kernel(dims, sources_in, *refs):
    peers, slots, blocks, picks, rows, width, bins_count, pay_rows = dims
    inc = peers - 1
    (w, w_t, head, bins, flags, aux, self2), refs = refs[:7], refs[7:]
    (own2, slope1, tiles, tiles_t, agg1_t, feat_t, hidden_t), refs = refs[:7], refs[7:]
    past_in, refs = refs[:inc], refs[inc:]
    (grad_hidden, keep, send, back), refs = refs[:4], refs[4:]
    sources, table, agg_t, gtab, pay, sem = refs
    g = lax.axis_index("grp")
    core = lax.axis_index("clus") % CORES
    device = lax.axis_index("clus") * peers + g
    nodes = blocks * rows
    scale = 1.0 / (nodes * peers)
    listed = pltpu.make_async_copy(sources_in, sources, sem)
    listed.start()
    table[pl.ds(0, blocks)] = own2[...]
    for step in range(1, peers):
        _, origin = partner(g, step, peers)
        table[pl.ds(blocks + origin * slots, slots)] = past_in[step - 1][...]
    remote = pl.ds(blocks, peers * slots)
    gtab[remote] = jnp.zeros((peers * slots, rows, width), F32)
    listed.wait()
    aggs = []
    for b in range(blocks):
        row = jnp.concatenate([tiles[b, k] for k in range(picks)], axis=1)
        agg = dot(row, gathered(table, sources, b, picks)).astype(BF16)
        aggs.append(agg)
        agg_t[:, b * rows : (b + 1) * rows] = agg.T
    pair = 2
    span = pair * rows
    step_col = lax.broadcasted_iota(jnp.int32, (bins_count, span), 0)
    loss = jnp.zeros((bins_count, span), F32)
    ghw = jnp.zeros((bins_count, width), F32)
    chunks = range(blocks // pair)
    at = [pl.ds(i * pair, pair) for i in chunks]
    gates = []
    for i in chunks:
        agg = jnp.concatenate(aggs[i * pair : (i + 1) * pair], axis=0)
        gates.append(gate_of(dot(agg, w[...]) + self2[pl.ds(i * span, span)]))
    hidden = [value.astype(BF16) for value, _ in gates]
    logits = [dot_by_transpose(head[...], hidden[i]) for i in chunks]
    glogs = []
    for i in chunks:
        counted = step_col <= bins[i]
        event = jnp.where(step_col == bins[i], flags[i].astype(F32), 0.0)
        tail = jnp.exp(-jnp.abs(logits[i]))
        soft = jnp.maximum(logits[i], 0.0) + jnp.log1p(tail)
        loss = loss + jnp.where(counted, soft, 0.0) - event * logits[i]
        chance = jnp.where(logits[i] >= 0.0, 1.0, tail) / (1.0 + tail)
        glogs.append((jnp.where(counted, chance, 0.0) - event).astype(BF16))
    grad_pres = [(transpose_dot(glogs[i], head[...]) * gates[i][1]).astype(BF16) for i in chunks]
    grad_aggs = []
    for i in chunks:
        onward = dot(grad_pres[i], w_t[...])
        grad_aggs.append(onward[:, :width].astype(BF16))
        own = onward[:, width:] + aux[at[i]].reshape(span, width).astype(F32)
        gtab[at[i]] = own.reshape(pair, rows, width)
    for i in chunks:
        ghw = ghw + dot(glogs[i], hidden[i])
    for b in range(blocks):
        part = grad_aggs[b // pair][(b % pair) * rows : (b % pair + 1) * rows]
        spread = dot(tiles_t[b], part)
        for k in range(picks):
            gtab[sources[k, b]] += spread[k * rows : (k + 1) * rows]
    back[...] = gtab[remote].astype(BF16)
    total = gtab[pl.ds(0, blocks)]
    grad_hidden[...] = total.astype(BF16)
    grad_first = (total.reshape(nodes, width) * slope1[...]).astype(BF16)
    grad_second = jnp.concatenate(grad_pres, axis=0)
    terms = (
        (agg1_t, grad_first),
        (feat_t, grad_first),
        (agg_t, grad_second),
        (hidden_t, grad_second),
    )
    for n, (left, grads) in enumerate(terms):
        pay[pl.ds(n * width, width)] = (dot(left[...], grads) * scale).astype(BF16)
    part = jnp.sum(loss) * scale
    high = part.astype(BF16).astype(F32)
    tail_rows = pay_rows - 4 * width - bins_count
    lane = lax.broadcasted_iota(jnp.int32, (tail_rows, width), 0) * width + lax.broadcasted_iota(
        jnp.int32, (tail_rows, width), 1
    )
    loss_rows = jnp.where(lane == 2 * device, high, 0.0) + jnp.where(
        lane == 2 * device + 1, part - high, 0.0
    )
    pay[pl.ds(4 * width, bins_count)] = (ghw * scale).astype(BF16)
    pay[pl.ds(4 * width + bins_count, tail_rows)] = loss_rows.astype(BF16)
    half = pay_rows // CORES
    keep[...] = pay[pl.ds(pl.multiple_of(core * half, 16), half)]
    send[...] = pay[pl.ds(pl.multiple_of((1 - core) * half, 16), half)]


def split_kernel(peers, kept, came, own, *outs):
    g = lax.axis_index("grp")

    def chunk(p):
        return (kept[p].astype(F32) + came[p].astype(F32)).astype(BF16)

    own[...] = chunk(g)
    for step in range(1, peers):
        peer, _ = partner(g, step, peers)
        outs[step - 1][...] = chunk(peer)


def store_kernel(hidden, grad_hidden, after, hidden_out, grad_hidden_out, token, sems):
    copies = [
        pltpu.make_async_copy(hidden, hidden_out, sems.at[0]),
        pltpu.make_async_copy(grad_hidden, grad_hidden_out, sems.at[1]),
    ]
    for copy in copies:
        copy.start()
    token[...] = jnp.zeros_like(token)
    for copy in copies:
        copy.wait()


def add_kernel(*refs):
    total = refs[0][...].astype(F32)
    for ref in refs[1:-1]:
        if ref.shape == total.shape:
            total = total + ref[...].astype(F32)
    refs[-1][...] = total.astype(BF16)


def join_kernel(peers, own, *refs):
    out = refs[-1]
    g = lax.axis_index("grp")
    out[g] = own[...]
    for step in range(1, peers):
        _, origin = partner(g, step, peers)
        out[origin] = refs[step - 1][...]


def finish_kernel(dims, mine, other, *outs):
    width, bins_count, pay_rows = dims
    pay = outs[-1]
    half = pay_rows // CORES
    core = lax.axis_index("clus") % CORES
    pay[pl.ds(pl.multiple_of(core * half, 16), half)] = mine[...]
    pay[pl.ds(pl.multiple_of((1 - core) * half, 16), half)] = other[...]
    for i in range(4):
        outs[i][...] = pay[pl.ds(i * width, width)].astype(F32)
    outs[4][...] = pay[pl.ds(4 * width, bins_count)].astype(F32)
    loss_rows = pay[pl.ds(4 * width + bins_count, pay_rows - 4 * width - bins_count)].astype(F32)
    outs[5][0, 0] = jnp.sum(loss_rows)


def back_kernel(peers, slots, blocks, back, after, *outs):
    g = lax.axis_index("grp")
    for step in range(1, peers):
        _, origin = partner(g, step, peers)
        outs[step - 1][...] = back[pl.ds(origin * slots, slots)]


def aux_kernel(peers, slots, blocks, send, *refs):
    back, out, token, total, lists, sem = refs[:-5], *refs[-5:]
    g = lax.axis_index("grp")
    listed = pltpu.make_async_copy(send, lists, sem)
    listed.start()
    total[...] = jnp.zeros_like(total)
    token[...] = jnp.zeros_like(token)
    listed.wait()
    for step in range(1, peers):
        peer, _ = partner(g, step, peers)
        for s in range(slots):
            total[lists[s, peer]] += back[step - 1][s].astype(F32)
    out[...] = total[pl.ds(0, blocks)].astype(BF16)


def shards(
    clus_count,
    peers,
    features,
    history,
    aux_history,
    tile_values,
    tile_sources,
    send_list,
    event_bins,
    event_flags,
    neigh_first,
    self_first,
    neigh_second,
    self_second,
    hazard_weight,
):
    blocks, picks, rows = tile_values.shape[2:5]
    width = features.shape[3]
    slots = send_list.shape[3]
    bins_count = hazard_weight.shape[1]
    devices = clus_count * peers
    chips_z = clus_count // CORES
    inc = peers - 1
    used = 4 * width + bins_count + -(-2 * devices // width)
    pay_rows = -(-used // (16 * CORES * peers)) * 16 * CORES * peers
    half = pay_rows // CORES
    chunk = half // peers
    block_shape = (blocks, rows, width)
    slot_shape = (slots, rows, width)
    routing = send_list[0, 0].T
    feat = features.reshape(block_shape)
    past = history.reshape(block_shape)
    params = pltpu.CompilerParams(vmem_limit_bytes=20 << 20)
    small = pltpu.CompilerParams(vmem_limit_bytes=4 << 20)

    def shape(dims, dtype=BF16):
        return jax.ShapeDtypeStruct(dims, dtype)

    def grp_pairs(step):
        return [(i, partner(i, step, peers)[0]) for i in range(peers)]

    def over_grp(value, step):
        return lax.ppermute(value, "grp", grp_pairs(step))

    def over_z(value, step):
        pairs = [
            (z * CORES + c, partner(z, step, chips_z)[0] * CORES + c)
            for z in range(chips_z)
            for c in range(CORES)
        ]
        return lax.ppermute(value, "clus", pairs)

    def over_core(value):
        return lax.ppermute(value, "clus", [(i, i ^ 1) for i in range(clus_count)])

    lists = (slots, peers)
    nodes = blocks * rows
    table = blocks + peers * slots
    tiles = tile_values[0, 0]
    sources = tile_sources[0, 0].T
    square = (width, width)
    turned = (width, nodes)
    packed = pl.pallas_call(
        functools.partial(pack_kernel, peers, slots, blocks),
        out_shape=[shape(slot_shape)] * (2 * inc) + [shape((8, 128), F32)],
        in_specs=[HBM] * 3,
        out_specs=[VMEM] * (2 * inc + 1),
        scratch_shapes=[
            pltpu.SMEM(lists, jnp.int32),
            pltpu.VMEM(block_shape, BF16),
            pltpu.VMEM(block_shape, BF16),
            pltpu.SemaphoreType.DMA((3,)),
        ],
        compiler_params=pltpu.CompilerParams(vmem_limit_bytes=PACK_LIMIT),
        name="pack",
    )(routing, feat, past)
    feat_in = [over_grp(packed[i], i + 1) for i in range(inc)]
    past_in = [over_grp(packed[inc + i], i + 1) for i in range(inc)]
    tiles_t, feat_t, feat = pl.pallas_call(
        functools.partial(prepare_kernel, (blocks, picks, rows)),
        out_shape=[
            shape((blocks, picks * rows, rows)),
            shape(turned),
            shape(block_shape),
        ],
        in_specs=[VMEM] * 3,
        out_specs=[VMEM] * 3,
        compiler_params=pltpu.CompilerParams(vmem_limit_bytes=PREP_LIMIT),
        cost_estimate=pl.CostEstimate(flops=10**9, bytes_accessed=10**7, transcendentals=0),
        name="prepare",
    )(feat, tiles, packed[2 * inc])

    pair_shape = (blocks // 2, 1, 2 * rows)
    own2, slope1, agg_t, hidden_t, self2, w, w_t, head, bins, flags = pl.pallas_call(
        functools.partial(first_kernel, (peers, slots, blocks, picks, rows, width)),
        out_shape=[
            shape(block_shape),
            shape((nodes, width), F32),
            shape(turned),
            shape(turned),
            shape((nodes, width), F32),
            shape(square),
            shape((width, 2 * width)),
            shape((bins_count, width)),
            shape(pair_shape, jnp.int32),
            shape(pair_shape, jnp.int32),
        ],
        in_specs=[HBM] + [VMEM] * (9 + inc),
        out_specs=[VMEM] * 10,
        scratch_shapes=[
            pltpu.VMEM((table, rows, width), BF16),
            pltpu.SMEM((picks, blocks), jnp.int32),
            pltpu.SemaphoreType.DMA,
        ],
        compiler_params=params,
        name="first_layer",
    )(
        sources,
        neigh_first,
        self_first,
        neigh_second,
        self_second,
        hazard_weight.T,
        event_bins.reshape(pair_shape),
        event_flags.reshape(pair_shape),
        feat,
        tiles,
        *feat_in,
    )
    grad_hidden, kept, sent, back = pl.pallas_call(
        functools.partial(
            second_kernel, (peers, slots, blocks, picks, rows, width, bins_count, pay_rows)
        ),
        out_shape=[
            shape(block_shape),
            shape((half, width)),
            shape((half, width)),
            shape((peers * slots, rows, width)),
        ],
        in_specs=[HBM] + [VMEM] * (14 + inc),
        out_specs=[VMEM] * 4,
        scratch_shapes=[
            pltpu.SMEM((picks, blocks), jnp.int32),
            pltpu.VMEM((table, rows, width), BF16),
            pltpu.VMEM(turned, BF16),
            pltpu.VMEM((table, rows, width), F32),
            pltpu.VMEM((pay_rows, width), BF16),
            pltpu.SemaphoreType.DMA,
        ],
        compiler_params=params,
        name="second_layer",
    )(
        sources,
        w,
        w_t,
        head,
        bins,
        flags,
        aux_history.reshape(block_shape),
        self2,
        own2,
        slope1,
        tiles,
        tiles_t,
        agg_t,
        feat_t,
        hidden_t,
        *past_in,
    )

    came = over_core(sent)
    parts = pl.pallas_call(
        functools.partial(split_kernel, peers),
        out_shape=[shape((chunk, width))] * peers,
        in_specs=[VMEM, VMEM],
        out_specs=[VMEM] * peers,
        compiler_params=small,
        name="split",
    )(kept.reshape(peers, chunk, width), came.reshape(peers, chunk, width))
    from_grp = [over_grp(parts[i], i) for i in range(1, peers)]

    def add(*values):
        return pl.pallas_call(
            add_kernel,
            out_shape=shape((chunk, width)),
            in_specs=[VMEM] * len(values),
            out_specs=VMEM,
            compiler_params=small,
            name="add",
        )(*values)

    hidden_first, grad_hidden, stored = pl.pallas_call(
        store_kernel,
        out_shape=[shape(block_shape), shape(block_shape), shape((8, 128), F32)],
        in_specs=[VMEM] * 3,
        out_specs=[HBM, HBM, VMEM],
        scratch_shapes=[pltpu.SemaphoreType.DMA((2,))],
        compiler_params=small,
        name="store",
    )(own2, grad_hidden, parts[0])
    mine = add(parts[0], *from_grp, stored)
    back = pl.pallas_call(
        functools.partial(back_kernel, peers, slots, blocks),
        out_shape=[shape(slot_shape)] * inc,
        in_specs=[VMEM, VMEM],
        out_specs=[VMEM] * inc,
        compiler_params=small,
        name="back",
    )(back, parts[0])
    came_back = [over_grp(back[i], i + 1) for i in range(inc)]
    new_aux, token = pl.pallas_call(
        functools.partial(aux_kernel, peers, slots, blocks),
        out_shape=[shape(block_shape), shape((8, 128), F32)],
        in_specs=[HBM] + [VMEM] * inc,
        out_specs=[VMEM] * 2,
        scratch_shapes=[
            pltpu.VMEM((blocks + 1, rows, width), F32),
            pltpu.SMEM(lists, jnp.int32),
            pltpu.SemaphoreType.DMA,
        ],
        compiler_params=small,
        cost_estimate=pl.CostEstimate(flops=AUX_FLOPS, bytes_accessed=10**6, transcendentals=0),
        name="aux",
    )(routing, *came_back)
    mine = add(mine, *[over_z(mine, i) for i in range(1, chips_z)])
    others = [over_grp(mine, i) for i in range(1, peers)]
    joined = pl.pallas_call(
        functools.partial(join_kernel, peers),
        out_shape=shape((peers, chunk, width)),
        in_specs=[VMEM] * (peers + 1),
        out_specs=VMEM,
        compiler_params=small,
        name="join",
    )(mine, *others, token).reshape(half, width)
    other_half = over_core(joined)
    grads = pl.pallas_call(
        functools.partial(finish_kernel, (width, bins_count, pay_rows)),
        out_shape=[shape(square, F32)] * 4 + [shape((bins_count, width), F32), shape((1, 1), F32)],
        in_specs=[VMEM] * 2,
        out_specs=[VMEM] * 5 + [SMEM],
        scratch_shapes=[pltpu.VMEM((pay_rows, width), BF16)],
        compiler_params=small,
        name="finish",
    )(joined, other_half)
    return (
        hidden_first.reshape(features.shape),
        grad_hidden.reshape(features.shape),
        new_aux.reshape(features.shape),
        *grads[:4],
        grads[4].T,
        grads[5][0, 0],
    )


def solution(mesh):
    split = P("clus", "grp")
    whole = P()
    return jax.shard_map(
        functools.partial(shards, mesh.shape["clus"], mesh.shape["grp"]),
        mesh=mesh,
        in_specs=(split,) * 8 + (whole,) * 5,
        out_specs=(split,) * 3 + (whole,) * 6,
        check_vma=False,
    )
```

```python
import functools

import jax
import jax.numpy as jnp
from jax import lax
from jax.experimental import pallas as pl
from jax.experimental.pallas import tpu as pltpu
from jax.sharding import PartitionSpec as P

BF16 = jnp.bfloat16
F32 = jnp.float32
VMEM = pl.BlockSpec(memory_space=pltpu.VMEM)
SMEM = pl.BlockSpec(memory_space=pltpu.SMEM)
HBM = pl.BlockSpec(memory_space=pltpu.HBM)
CORES = 2
LANES = 128
PACK_LIMIT = 53 << 20
PREP_LIMIT = 4 << 20
AUX_FLOPS = 10**6


def dot(former, latter):
    return jnp.dot(former, latter, preferred_element_type=F32)


def transpose_dot(former, latter):
    return lax.dot_general(former, latter, (((0,), (0,)), ((), ())), preferred_element_type=F32)


def dot_by_transpose(former, latter):
    return lax.dot_general(former, latter, (((1,), (1,)), ((), ())), preferred_element_type=F32)


def partner(index, step, count):
    if count & (count - 1) == 0:
        return index ^ step, index ^ step
    return (index + step) % count, (index + count - step) % count


def pack_kernel(peers, slots, blocks, send, feat_in, past_in, *refs):
    outs, (token, lists, feat, past, sems) = refs[:-5], refs[-5:]
    g = lax.axis_index("grp")
    pairs = ((send, lists), (feat_in, feat), (past_in, past))
    copies = [pltpu.make_async_copy(src, dst, sems.at[i]) for i, (src, dst) in enumerate(pairs)]
    for copy in copies:
        copy.start()
    token[...] = jnp.zeros_like(token)
    copies[0].wait()
    for which, values in enumerate((feat, past)):
        copies[1 + which].wait()
        for step in range(1, peers):
            peer, _ = partner(g, step, peers)
            for s in range(slots):
                block = jnp.minimum(lists[s, peer], blocks - 1)
                outs[which * (peers - 1) + step - 1][s] = values[block]


def prepare_kernel(dims, feat, tiles, token, tiles_t, feat_t, feat_kept):
    blocks, picks, rows = dims
    feat_kept[...] = feat[...]
    for b in range(blocks):
        feat_t[:, b * rows : (b + 1) * rows] = feat[b].T
    for b in range(blocks):
        for k in range(picks):
            tiles_t[b, k * rows : (k + 1) * rows] = tiles[b, k].T


def gathered(table, sources, b, picks):
    return jnp.concatenate([table[sources[k, b]] for k in range(picks)], axis=0)


def gate_of(pre):
    gate = 0.5 * jnp.tanh(0.5 * pre) + 0.5
    value = pre * gate
    return value, gate + value * (1.0 - gate)


def first_kernel(dims, sources_in, wn, ws, wn_next, ws_next, head, bins, flags, feat, tiles, *refs):
    peers, slots, blocks, picks, rows, width = dims
    inc = peers - 1
    feat_in, refs = refs[:inc], refs[inc:]
    own2, slope1, agg_t, hidden_t, self2, w, w_t, head_kept, bins_kept, flags_kept = refs[:10]
    table, sources, sem = refs[10:]
    g = lax.axis_index("grp")
    listed = pltpu.make_async_copy(sources_in, sources, sem)
    listed.start()
    table[pl.ds(0, blocks)] = feat[...]
    for step in range(1, peers):
        _, origin = partner(g, step, peers)
        table[pl.ds(blocks + origin * slots, slots)] = feat_in[step - 1][...]
    head_kept[...] = head[...]
    bins_kept[...] = bins[...]
    flags_kept[...] = flags[...]
    w[...] = wn_next[...]
    w_t[:, :width] = wn_next[...].T
    w_t[:, width:] = ws_next[...].T
    listed.wait()
    aggs = []
    for b in range(blocks):
        row = jnp.concatenate([tiles[b, k] for k in range(picks)], axis=1)
        agg = dot(row, gathered(table, sources, b, picks)).astype(BF16)
        aggs.append(agg)
        agg_t[:, b * rows : (b + 1) * rows] = agg.T
    both_w = jnp.concatenate([wn[...], ws[...]], axis=0)
    pair = 2
    span = pair * rows
    for i in range(blocks // pair):
        at = pl.ds(i * span, span)
        nodes_feat = table[pl.ds(i * pair, pair)].reshape(span, width)
        both = jnp.concatenate(
            [jnp.concatenate(aggs[i * pair : (i + 1) * pair], axis=0), nodes_feat], axis=1
        )
        value, slope = gate_of(dot(both, both_w))
        slope1[at] = slope
        hidden = value.astype(BF16)
        own2[pl.ds(i * pair, pair)] = hidden.reshape(pair, rows, width)
        hidden_t[:, at] = hidden.T
        self2[at] = dot(hidden, ws_next[...])


def second_kernel(dims, sources_in, *refs):
    peers, slots, blocks, picks, rows, width, bins_count, pay_rows = dims
    inc = peers - 1
    (w, w_t, head, bins, flags, aux, self2), refs = refs[:7], refs[7:]
    (own2, slope1, tiles, tiles_t, agg1_t, feat_t, hidden_t), refs = refs[:7], refs[7:]
    past_in, refs = refs[:inc], refs[inc:]
    (grad_hidden, keep, send, back), refs = refs[:4], refs[4:]
    sources, table, agg_t, gtab, pay, sem = refs
    g = lax.axis_index("grp")
    core = lax.axis_index("clus") % CORES
    device = lax.axis_index("clus") * peers + g
    nodes = blocks * rows
    scale = 1.0 / (nodes * peers)
    listed = pltpu.make_async_copy(sources_in, sources, sem)
    listed.start()
    table[pl.ds(0, blocks)] = own2[...]
    for step in range(1, peers):
        _, origin = partner(g, step, peers)
        table[pl.ds(blocks + origin * slots, slots)] = past_in[step - 1][...]
    remote = pl.ds(blocks, peers * slots)
    gtab[remote] = jnp.zeros((peers * slots, rows, width), F32)
    listed.wait()
    aggs = []
    for b in range(blocks):
        row = jnp.concatenate([tiles[b, k] for k in range(picks)], axis=1)
        agg = dot(row, gathered(table, sources, b, picks)).astype(BF16)
        aggs.append(agg)
        agg_t[:, b * rows : (b + 1) * rows] = agg.T
    pair = 2
    span = pair * rows
    step_col = lax.broadcasted_iota(jnp.int32, (bins_count, span), 0)
    loss = jnp.zeros((bins_count, span), F32)
    ghw = jnp.zeros((bins_count, width), F32)
    chunks = range(blocks // pair)
    at = [pl.ds(i * pair, pair) for i in chunks]
    gates = []
    for i in chunks:
        agg = jnp.concatenate(aggs[i * pair : (i + 1) * pair], axis=0)
        gates.append(gate_of(dot(agg, w[...]) + self2[pl.ds(i * span, span)]))
    hidden = [value.astype(BF16) for value, _ in gates]
    logits = [dot_by_transpose(head[...], hidden[i]) for i in chunks]
    glogs = []
    for i in chunks:
        counted = step_col <= bins[i]
        event = jnp.where(step_col == bins[i], flags[i].astype(F32), 0.0)
        tail = jnp.exp(-jnp.abs(logits[i]))
        soft = jnp.maximum(logits[i], 0.0) + jnp.log1p(tail)
        loss = loss + jnp.where(counted, soft, 0.0) - event * logits[i]
        chance = jnp.where(logits[i] >= 0.0, 1.0, tail) / (1.0 + tail)
        glogs.append((jnp.where(counted, chance, 0.0) - event).astype(BF16))
    grad_pres = [(transpose_dot(glogs[i], head[...]) * gates[i][1]).astype(BF16) for i in chunks]
    grad_aggs = []
    for i in chunks:
        onward = dot(grad_pres[i], w_t[...])
        grad_aggs.append(onward[:, :width].astype(BF16))
        own = onward[:, width:] + aux[at[i]].reshape(span, width).astype(F32)
        gtab[at[i]] = own.reshape(pair, rows, width)
    for i in chunks:
        ghw = ghw + dot(glogs[i], hidden[i])
    for b in range(blocks):
        part = grad_aggs[b // pair][(b % pair) * rows : (b % pair + 1) * rows]
        spread = dot(tiles_t[b], part)
        for k in range(picks):
            gtab[sources[k, b]] += spread[k * rows : (k + 1) * rows]
    back[...] = gtab[remote].astype(BF16)
    total = gtab[pl.ds(0, blocks)]
    grad_hidden[...] = total.astype(BF16)
    grad_first = (total.reshape(nodes, width) * slope1[...]).astype(BF16)
    grad_second = jnp.concatenate(grad_pres, axis=0)
    terms = (
        (agg1_t, grad_first),
        (feat_t, grad_first),
        (agg_t, grad_second),
        (hidden_t, grad_second),
    )
    def put(at, values):
        for i in range(width // LANES):
            count = values.shape[0]
            pay[pl.ds(at + i * count, count)] = values[:, i * LANES : (i + 1) * LANES]

    folds = width // LANES
    for n, (left, grads) in enumerate(terms):
        put(n * width * folds, (dot(left[...], grads) * scale).astype(BF16))
    part = jnp.sum(loss) * scale
    high = part.astype(BF16).astype(F32)
    tail_rows = pay_rows - (4 * width + bins_count) * folds
    lane = lax.broadcasted_iota(jnp.int32, (tail_rows, LANES), 0) * LANES + lax.broadcasted_iota(
        jnp.int32, (tail_rows, LANES), 1
    )
    loss_rows = jnp.where(lane == 2 * device, high, 0.0) + jnp.where(
        lane == 2 * device + 1, part - high, 0.0
    )
    put(4 * width * folds, (ghw * scale).astype(BF16))
    pay[pl.ds((4 * width + bins_count) * folds, tail_rows)] = loss_rows.astype(BF16)
    half = pay_rows // CORES
    keep[...] = pay[pl.ds(pl.multiple_of(core * half, 16), half)]
    send[...] = pay[pl.ds(pl.multiple_of((1 - core) * half, 16), half)]


def split_kernel(peers, kept, came, own, *outs):
    g = lax.axis_index("grp")

    def chunk(p):
        return (kept[p].astype(F32) + came[p].astype(F32)).astype(BF16)

    own[...] = chunk(g)
    for step in range(1, peers):
        peer, _ = partner(g, step, peers)
        outs[step - 1][...] = chunk(peer)


def store_kernel(hidden, grad_hidden, after, hidden_out, grad_hidden_out, token, sems):
    copies = [
        pltpu.make_async_copy(hidden, hidden_out, sems.at[0]),
        pltpu.make_async_copy(grad_hidden, grad_hidden_out, sems.at[1]),
    ]
    for copy in copies:
        copy.start()
    token[...] = jnp.zeros_like(token)
    for copy in copies:
        copy.wait()


def add_kernel(*refs):
    total = refs[0][...].astype(F32)
    for ref in refs[1:-1]:
        if ref.shape == total.shape:
            total = total + ref[...].astype(F32)
    refs[-1][...] = total.astype(BF16)


def join_kernel(peers, own, *refs):
    out = refs[-1]
    g = lax.axis_index("grp")
    out[g] = own[...]
    for step in range(1, peers):
        _, origin = partner(g, step, peers)
        out[origin] = refs[step - 1][...]


def finish_kernel(dims, mine, other, *outs):
    width, bins_count, pay_rows = dims
    pay = outs[-1]
    half = pay_rows // CORES
    core = lax.axis_index("clus") % CORES
    pay[pl.ds(pl.multiple_of(core * half, 16), half)] = mine[...]
    pay[pl.ds(pl.multiple_of((1 - core) * half, 16), half)] = other[...]
    folds = width // LANES

    def get(at, count):
        parts = [pay[pl.ds(at + i * count, count)] for i in range(folds)]
        return jnp.concatenate(parts, axis=1).astype(F32)

    for i in range(4):
        outs[i][...] = get(i * width * folds, width)
    outs[4][...] = get(4 * width * folds, bins_count)
    used = (4 * width + bins_count) * folds
    loss_rows = pay[pl.ds(used, pay_rows - used)].astype(F32)
    outs[5][0, 0] = jnp.sum(loss_rows)


def back_kernel(peers, slots, blocks, back, after, *outs):
    g = lax.axis_index("grp")
    for step in range(1, peers):
        _, origin = partner(g, step, peers)
        outs[step - 1][...] = back[pl.ds(origin * slots, slots)]


def aux_kernel(peers, slots, blocks, send, *refs):
    back, out, token, total, lists, sem = refs[:-5], *refs[-5:]
    g = lax.axis_index("grp")
    listed = pltpu.make_async_copy(send, lists, sem)
    listed.start()
    total[...] = jnp.zeros_like(total)
    token[...] = jnp.zeros_like(token)
    listed.wait()
    for step in range(1, peers):
        peer, _ = partner(g, step, peers)
        for s in range(slots):
            total[lists[s, peer]] += back[step - 1][s].astype(F32)
    out[...] = total[pl.ds(0, blocks)].astype(BF16)


def shards(
    clus_count,
    peers,
    features,
    history,
    aux_history,
    tile_values,
    tile_sources,
    send_list,
    event_bins,
    event_flags,
    neigh_first,
    self_first,
    neigh_second,
    self_second,
    hazard_weight,
):
    blocks, picks, rows = tile_values.shape[2:5]
    width = features.shape[3]
    slots = send_list.shape[3]
    bins_count = hazard_weight.shape[1]
    devices = clus_count * peers
    chips_z = clus_count // CORES
    inc = peers - 1
    used = (4 * width + bins_count) * (width // LANES) + -(-2 * devices // LANES)
    pay_rows = -(-used // (16 * CORES * peers)) * 16 * CORES * peers
    half = pay_rows // CORES
    chunk = half // peers
    block_shape = (blocks, rows, width)
    slot_shape = (slots, rows, width)
    routing = send_list[0, 0].T
    feat = features.reshape(block_shape)
    past = history.reshape(block_shape)
    params = pltpu.CompilerParams(vmem_limit_bytes=20 << 20)
    small = pltpu.CompilerParams(vmem_limit_bytes=4 << 20)

    def shape(dims, dtype=BF16):
        return jax.ShapeDtypeStruct(dims, dtype)

    def grp_pairs(step):
        return [(i, partner(i, step, peers)[0]) for i in range(peers)]

    def over_grp(value, step):
        return lax.ppermute(value, "grp", grp_pairs(step))

    def over_z(value, step):
        pairs = [
            (z * CORES + c, partner(z, step, chips_z)[0] * CORES + c)
            for z in range(chips_z)
            for c in range(CORES)
        ]
        return lax.ppermute(value, "clus", pairs)

    def over_core(value):
        return lax.ppermute(value, "clus", [(i, i ^ 1) for i in range(clus_count)])

    lists = (slots, peers)
    nodes = blocks * rows
    table = blocks + peers * slots
    tiles = tile_values[0, 0]
    sources = tile_sources[0, 0].T
    square = (width, width)
    turned = (width, nodes)
    packed = pl.pallas_call(
        functools.partial(pack_kernel, peers, slots, blocks),
        out_shape=[shape(slot_shape)] * (2 * inc) + [shape((8, 128), F32)],
        in_specs=[HBM] * 3,
        out_specs=[VMEM] * (2 * inc + 1),
        scratch_shapes=[
            pltpu.SMEM(lists, jnp.int32),
            pltpu.VMEM(block_shape, BF16),
            pltpu.VMEM(block_shape, BF16),
            pltpu.SemaphoreType.DMA((3,)),
        ],
        compiler_params=pltpu.CompilerParams(vmem_limit_bytes=PACK_LIMIT),
        name="pack",
    )(routing, feat, past)
    feat_in = [over_grp(packed[i], i + 1) for i in range(inc)]
    past_in = [over_grp(packed[inc + i], i + 1) for i in range(inc)]
    tiles_t, feat_t, feat = pl.pallas_call(
        functools.partial(prepare_kernel, (blocks, picks, rows)),
        out_shape=[
            shape((blocks, picks * rows, rows)),
            shape(turned),
            shape(block_shape),
        ],
        in_specs=[VMEM] * 3,
        out_specs=[VMEM] * 3,
        compiler_params=pltpu.CompilerParams(vmem_limit_bytes=PREP_LIMIT),
        cost_estimate=pl.CostEstimate(flops=10**9, bytes_accessed=10**7, transcendentals=0),
        name="prepare",
    )(feat, tiles, packed[2 * inc])

    pair_shape = (blocks // 2, 1, 2 * rows)
    own2, slope1, agg_t, hidden_t, self2, w, w_t, head, bins, flags = pl.pallas_call(
        functools.partial(first_kernel, (peers, slots, blocks, picks, rows, width)),
        out_shape=[
            shape(block_shape),
            shape((nodes, width), F32),
            shape(turned),
            shape(turned),
            shape((nodes, width), F32),
            shape(square),
            shape((width, 2 * width)),
            shape((bins_count, width)),
            shape(pair_shape, jnp.int32),
            shape(pair_shape, jnp.int32),
        ],
        in_specs=[HBM] + [VMEM] * (9 + inc),
        out_specs=[VMEM] * 10,
        scratch_shapes=[
            pltpu.VMEM((table, rows, width), BF16),
            pltpu.SMEM((picks, blocks), jnp.int32),
            pltpu.SemaphoreType.DMA,
        ],
        compiler_params=params,
        name="first_layer",
    )(
        sources,
        neigh_first,
        self_first,
        neigh_second,
        self_second,
        hazard_weight.T,
        event_bins.reshape(pair_shape),
        event_flags.reshape(pair_shape),
        feat,
        tiles,
        *feat_in,
    )
    grad_hidden, kept, sent, back = pl.pallas_call(
        functools.partial(
            second_kernel, (peers, slots, blocks, picks, rows, width, bins_count, pay_rows)
        ),
        out_shape=[
            shape(block_shape),
            shape((half, LANES)),
            shape((half, LANES)),
            shape((peers * slots, rows, width)),
        ],
        in_specs=[HBM] + [VMEM] * (14 + inc),
        out_specs=[VMEM] * 4,
        scratch_shapes=[
            pltpu.SMEM((picks, blocks), jnp.int32),
            pltpu.VMEM((table, rows, width), BF16),
            pltpu.VMEM(turned, BF16),
            pltpu.VMEM((table, rows, width), F32),
            pltpu.VMEM((pay_rows, LANES), BF16),
            pltpu.SemaphoreType.DMA,
        ],
        compiler_params=params,
        name="second_layer",
    )(
        sources,
        w,
        w_t,
        head,
        bins,
        flags,
        aux_history.reshape(block_shape),
        self2,
        own2,
        slope1,
        tiles,
        tiles_t,
        agg_t,
        feat_t,
        hidden_t,
        *past_in,
    )

    came = over_core(sent)
    parts = pl.pallas_call(
        functools.partial(split_kernel, peers),
        out_shape=[shape((chunk, LANES))] * peers,
        in_specs=[VMEM, VMEM],
        out_specs=[VMEM] * peers,
        compiler_params=small,
        name="split",
    )(kept.reshape(peers, chunk, LANES), came.reshape(peers, chunk, LANES))
    from_grp = [over_grp(parts[i], i) for i in range(1, peers)]

    def add(*values):
        return pl.pallas_call(
            add_kernel,
            out_shape=shape((chunk, LANES)),
            in_specs=[VMEM] * len(values),
            out_specs=VMEM,
            compiler_params=small,
            name="add",
        )(*values)

    hidden_first, grad_hidden, stored = pl.pallas_call(
        store_kernel,
        out_shape=[shape(block_shape), shape(block_shape), shape((8, 128), F32)],
        in_specs=[VMEM] * 3,
        out_specs=[HBM, HBM, VMEM],
        scratch_shapes=[pltpu.SemaphoreType.DMA((2,))],
        compiler_params=small,
        name="store",
    )(own2, grad_hidden, parts[0])
    mine = add(parts[0], *from_grp, stored)
    back = pl.pallas_call(
        functools.partial(back_kernel, peers, slots, blocks),
        out_shape=[shape(slot_shape)] * inc,
        in_specs=[VMEM, VMEM],
        out_specs=[VMEM] * inc,
        compiler_params=small,
        name="back",
    )(back, parts[0])
    came_back = [over_grp(back[i], i + 1) for i in range(inc)]
    new_aux, token = pl.pallas_call(
        functools.partial(aux_kernel, peers, slots, blocks),
        out_shape=[shape(block_shape), shape((8, 128), F32)],
        in_specs=[HBM] + [VMEM] * inc,
        out_specs=[VMEM] * 2,
        scratch_shapes=[
            pltpu.VMEM((blocks + 1, rows, width), F32),
            pltpu.SMEM(lists, jnp.int32),
            pltpu.SemaphoreType.DMA,
        ],
        compiler_params=small,
        cost_estimate=pl.CostEstimate(flops=AUX_FLOPS, bytes_accessed=10**6, transcendentals=0),
        name="aux",
    )(routing, *came_back)
    mine = add(mine, *[over_z(mine, i) for i in range(1, chips_z)])
    others = [over_grp(mine, i) for i in range(1, peers)]
    joined = pl.pallas_call(
        functools.partial(join_kernel, peers),
        out_shape=shape((peers, chunk, LANES)),
        in_specs=[VMEM] * (peers + 1),
        out_specs=VMEM,
        compiler_params=small,
        name="join",
    )(mine, *others, token).reshape(half, LANES)
    other_half = over_core(joined)
    grads = pl.pallas_call(
        functools.partial(finish_kernel, (width, bins_count, pay_rows)),
        out_shape=[shape(square, F32)] * 4 + [shape((bins_count, width), F32), shape((1, 1), F32)],
        in_specs=[VMEM] * 2,
        out_specs=[VMEM] * 5 + [SMEM],
        scratch_shapes=[pltpu.VMEM((pay_rows, LANES), BF16)],
        compiler_params=small,
        name="finish",
    )(joined, other_half)
    return (
        hidden_first.reshape(features.shape),
        grad_hidden.reshape(features.shape),
        new_aux.reshape(features.shape),
        *grads[:4],
        grads[4].T,
        grads[5][0, 0],
    )


def solution(mesh):
    split = P("clus", "grp")
    whole = P()
    return jax.shard_map(
        functools.partial(shards, mesh.shape["clus"], mesh.shape["grp"]),
        mesh=mesh,
        in_specs=(split,) * 8 + (whole,) * 5,
        out_specs=(split,) * 3 + (whole,) * 6,
        check_vma=False,
    )
```
